32 devices in a mesh: occ: 8 (over z, y), ao: 4 (over x, core).
Axes of the slice: x: 2, y: 2, z: 4, core: 2. Of those that a mesh axis runs over, the one named last changes fastest.
Arguments:
- amplitudes: bfloat16 [256, 256, 256], P('occ', None, 'ao'), may hold values from -6 to 6
- orbitals: bfloat16 [512, 256], replicated, may hold values from -0.375 to 0.375
- tiles: bfloat16 [512, 512, 512], P('occ', None, 'ao'), may hold values from -0.125 to 0.125
- tile_count: int32 [8], replicated, may hold values from 1 to 64, 256 in all
- tile_row: int32 [512], replicated, may hold values from 0 to 63
- tile_src: int32 [512, 1], replicated, may hold values from 0 to 7; in each aligned block of 64 rows (0 to 63, 64 to 127, ...) at most 8 rows name the same one
- tile_sub: int32 [512], replicated, may hold values from 0 to 63
Outputs:
- sigma_out: bfloat16 [256, 256, 256], P('occ', None, 'ao')
The draws below stay inside these ranges and needn't reach their ends.
Inputs may be any that keep to these rules, and one draw needn't show every extreme that they name: `tile_count`: each occ index owns between 1 and 64 live slots, the first ones of its 64 slots; some index owns exactly 64. `tile_src`: among the 64 slots of one owner no source index is named more than 8 times, and some owner names one source exactly 8 times.
All inputs are finite; a program needn't handle non-finite values.
Results may differ from the reference program's by a relative error of at most 0.024.
Values may be sent and summed in bfloat16 or wider, within the bound.
No kernel may reach another device: no remote copies, remote signals or barrier semaphores. Data moves between devices by JAX's collectives and lax.ppermute only.
A program may use at most 128 MiB of HBM per device.

```python
import math
import jax
import jax.numpy as jnp
import numpy as np
from jax import lax

NOCC = 256
NVIR = 256
NAO = 512
CAP = 64
TILE_SLOTS = 512
TILES = 256
ROWBLK = 64
QMAX = 8
N_OCC = 8


def touch_ends(values, key, smallest, high):
    place = [jax.random.randint(jax.random.fold_in(key, axis), (), 0, length) for axis, length in enumerate(values.shape)]
    widest = values.shape.index(max(values.shape))
    neighbour = place[:widest] + [(place[widest] + 1) % values.shape[widest]] + place[widest + 1:]
    return values.at[tuple(place)].set(smallest).at[tuple(neighbour)].set(high)


def block_levels(own_key, shape, pieces, low, high):
    def one(axis_at, parts):
        steps = jax.random.uniform(jax.random.fold_in(jax.random.fold_in(own_key, 6), axis_at), (parts,), jnp.float32, low / len(pieces), high / len(pieces))
        return jnp.repeat(jnp.exp(steps), shape[axis_at] // parts).reshape((-1,) + (1,) * (len(shape) - axis_at - 1))

    gain = one(*pieces[0])
    for cut in pieces[1:]:
        gain = gain * one(*cut)
    return gain


def length_profile(number_of, total, most, slope):
    weights = [(1 << 20) // math.isqrt(grade ** slope) + 1 for grade in range(2, number_of + 1)]
    surplus, counts = total - most - (number_of - 1), [1] * (number_of - 1)
    while surplus > 0:
        candidates = [i for i in range(number_of - 1) if counts[i] < most]
        whole, left = sum([weights[i] for i in candidates]), surplus
        for i in candidates:
            addition = min(most - counts[i], max(1, left * weights[i] // whole), surplus)
            counts[i] = counts[i] + addition
            surplus = surplus - addition
    return np.array([most] + counts)


def uneven(key, count, total, limit, lean):
    if count == 2:
        one = jax.random.randint(key, (), max(1, total - limit), min(limit, total - 1) + 1)
        return jnp.stack([one, total - one])
    sizes = jnp.asarray(length_profile(count, total, limit, lean), jnp.int32)
    couples = (count - 1) // 2
    source_of, taker = sizes[1:1 + 2 * couples:2], sizes[2:2 + 2 * couples:2]
    room = jnp.minimum(source_of - 1, limit - taker)
    shifted = jax.random.randint(jax.random.fold_in(key, 1), (couples,), 0, 1 << 20) % (room + 1)
    sizes = sizes.at[1:1 + 2 * couples:2].set(source_of - shifted).at[2:2 + 2 * couples:2].set(taker + shifted)
    return sizes[jax.random.permutation(jax.random.fold_in(key, 2), count)]


def routed_block(stream_key, own, number, rows, count, top, reach, lean):
    order = jax.random.permutation(stream_key, count)
    crowded, common = portions_of(count, rows * top, reach, lean, True), portions_of(count, rows * top, reach, lean, False)
    places = jnp.arange(count)

    def named(sizes, offset_by):
        used = int((sizes > 0).sum())
        fixed = max(1, used // 4)
        shifted = fixed + (places - fixed + offset_by * (used - fixed)) % max(1, count - fixed)
        return jnp.zeros((count,), jnp.int32).at[order[jnp.where(places < fixed, places, shifted)]].set(jnp.asarray(sizes, jnp.int32))

    sizes = jnp.where(number % 4 == 0, named(crowded, number // 4), named(common, number - number // 4 - 1))
    mixed = jax.random.permutation(jax.random.fold_in(own, 3), count)
    giver, receiver = mixed[0:count // 2 * 2:2], mixed[1:count // 2 * 2:2]
    slack = jnp.minimum(sizes[giver] - 1, reach - sizes[receiver]) // 2
    slack = jnp.where((giver == order[0]) | (receiver == order[0]) | (sizes[receiver] == 0), 0, jnp.maximum(slack, 0))
    shifted = jax.random.randint(jax.random.fold_in(own, 4), (count // 2,), 0, 1 << 20) % (slack + 1)
    sizes = sizes.at[giver].add(-shifted).at[receiver].add(shifted)
    items = jnp.searchsorted(jnp.cumsum(sizes), jnp.arange(rows * top), side="right").astype(jnp.int32)
    grid = items.reshape(top, rows).T
    grid = grid[jax.random.permutation(jax.random.fold_in(own, 1), rows)]
    offset_by = jax.random.randint(jax.random.fold_in(own, 2), (rows, 1), 0, top)
    return jnp.take_along_axis(grid, (jnp.arange(top)[None, :] + offset_by) % top, axis=1)


def portions_of(count, total, most, skew, full):
    weights = [(1 << 20) // math.isqrt(rank ** skew) + 1 for rank in range(1, count + 1)]
    largest = most if full else min(most, max(-(-total // count), total * weights[0] // sum(weights)))
    least = 1 if total - largest >= count - 1 else 0
    holding, rest = [largest] + [least] * (count - 1), total - largest - least * (count - 1)
    while rest > 0:
        free = [i for i in range(1, count) if holding[i] < largest] or [i for i in range(1, count) if holding[i] < most]
        pool, remaining = sum([weights[i] for i in free]), rest
        for i in free:
            more = min(most - holding[i], max(1, remaining * weights[i] // pool), rest)
            holding[i] = holding[i] + more
            rest = rest - more
    return np.array(holding)


def noise(key, shape, scale, bound, pieces=(), kind=jnp.bfloat16):
    values = scale * jax.random.normal(key, shape, jnp.float32)
    if pieces:
        values = values * block_levels(key, shape, pieces, -0.22, 0.18)
    return jnp.clip(values, -bound, bound).astype(kind)


def setup_inputs(seed: int = 0) -> dict:
    seeds = jax.random.split(jax.random.key(seed), 8)
    amplitudes = noise(seeds[0], (NOCC, NVIR, NVIR), 1.0, 6.0, ((0, 8), (2, 4)))
    orbitals = noise(seeds[1], (NAO, NVIR), NVIR ** -0.5, 0.375)
    tiles = noise(seeds[2], (TILE_SLOTS, NAO, NAO), (4 * NAO) ** -0.5, 0.125, ((0, 8), (2, 4)))
    tile_count = uneven(seeds[3], N_OCC, TILES, CAP, 2).astype(jnp.int32)
    tile_row = touch_ends(jax.random.randint(seeds[4], (TILE_SLOTS,), 0, ROWBLK), jax.random.fold_in(seeds[4], 1), 0, ROWBLK - 1).astype(jnp.int32)
    tile_src_keys = jax.random.split(jax.random.fold_in(seeds[5], 1), TILE_SLOTS // CAP)
    tile_src_turns = jax.random.permutation(jax.random.fold_in(seeds[5], 3), TILE_SLOTS // CAP)
    tile_src = jax.vmap(lambda own, number: routed_block(jax.random.fold_in(seeds[5], 2), own, number, CAP, N_OCC, 1, QMAX, 1))(tile_src_keys, tile_src_turns).reshape((TILE_SLOTS, 1))
    tile_sub = touch_ends(jax.random.randint(seeds[6], (TILE_SLOTS,), 0, ROWBLK), jax.random.fold_in(seeds[6], 1), 0, ROWBLK - 1).astype(jnp.int32)
    return {"amplitudes": amplitudes, "orbitals": orbitals, "tiles": tiles, "tile_count": tile_count, "tile_row": tile_row, "tile_src": tile_src, "tile_sub": tile_sub}


def reference(amplitudes, orbitals, tiles, tile_count, tile_row, tile_src, tile_sub):
    coeffs = orbitals.astype(jnp.float32)
    half_pairs = jnp.einsum('icd,nd->icn', amplitudes.astype(jnp.float32), coeffs).astype(jnp.bfloat16)
    pair_rows = jnp.einsum('mc,icn->imn', coeffs, half_pairs.astype(jnp.float32)).astype(jnp.bfloat16)
    pair_values = pair_rows.astype(jnp.float32)

    def add_tile(running, slot_id):
        owner = (slot_id // CAP).astype(jnp.int32)
        is_live = (slot_id % CAP) < tile_count[owner]
        row_block = (owner * ROWBLK + tile_row[slot_id]).astype(jnp.int32)
        col_block = (tile_src[slot_id, 0] * ROWBLK + tile_sub[slot_id]).astype(jnp.int32)

        def accumulate(current):
            column = lax.dynamic_slice_in_dim(pair_values, col_block, 1, 1)[:, 0, :]
            tile_f32 = lax.dynamic_index_in_dim(tiles, slot_id, 0, keepdims=False).astype(jnp.float32)
            term = jnp.dot(column, tile_f32.T, preferred_element_type=jnp.float32)
            before = lax.dynamic_slice_in_dim(current, row_block, 1, 1)
            return lax.dynamic_update_slice_in_dim(current, before + term[:, None, :], row_block, 1)

        def keep(current):
            return current

        return lax.cond(is_live, accumulate, keep, running), None

    start = jnp.zeros((NOCC, NAO, NAO), jnp.float32)
    ladder, _ = lax.scan(add_tile, start, jnp.arange(TILE_SLOTS, dtype=jnp.int32))
    ladder = ladder.astype(jnp.bfloat16)
    mixed = jnp.einsum('la,ils->ias', coeffs, ladder.astype(jnp.float32)).astype(jnp.bfloat16)
    sigma_out = jnp.einsum('ias,sb->iab', mixed.astype(jnp.float32), coeffs).astype(jnp.bfloat16)
    return sigma_out
```

```python
import jax
import jax.numpy as jnp
from jax import lax
from jax.sharding import PartitionSpec as P

CHUNKS = 4


def shards(amplitudes, orbitals, tiles, tile_count, tile_row, tile_src, tile_sub):
    nodes = lax.axis_size("occ")
    own = lax.axis_index("occ")
    parts = lax.axis_size("ao")
    part = lax.axis_index("ao")
    core, side = part % 2, part // 2
    near = [(q, q ^ 1) for q in range(parts)]
    far = [(q, (q + 2) % parts) for q in range(parts)]
    local_occ, vir, vir_part = amplitudes.shape
    ao_count = orbitals.shape[0]
    nu_part = tiles.shape[2]
    slots = tiles.shape[0]
    half = slots // 2
    step = half // CHUNKS
    blocks = ao_count // nodes
    f32, bf16 = jnp.float32, jnp.bfloat16
    pick = lax.dynamic_slice_in_dim

    def join(mine, other, axis):
        return jnp.where(
            core == 0,
            jnp.concatenate([mine, other], axis),
            jnp.concatenate([other, mine], axis),
        )

    def mine_of(table):
        return pick(table.reshape(nodes, slots), core * half, half, 1)

    source = mine_of(tile_src[:, 0]) * blocks + mine_of(tile_sub)
    target = jnp.arange(nodes, dtype=jnp.int32)[:, None] * blocks + mine_of(tile_row)
    place = core * half + jnp.arange(half, dtype=jnp.int32)
    live = place[None, :] < tile_count[:, None]
    source_rows = jnp.take(orbitals, source, axis=0)
    target_rows = jnp.where(live[:, :, None], jnp.take(orbitals, target, axis=0), 0)

    paired = join(amplitudes, lax.ppermute(amplitudes, "ao", near), 2)
    nu_rows = pick(orbitals, side * 2 * nu_part, 2 * nu_part, 0)
    side_vir = 2 * vir_part
    far_side = (side + 1) % (parts // 2)

    dressed = []
    for n in range(CHUNKS):
        first = pick(tiles, core * half + n * step, step, 0)
        second = pick(tiles, (1 - core) * half + n * step, step, 0)
        keep = jnp.einsum("sb,tsn->tbn", orbitals, first, preferred_element_type=f32).astype(bf16)
        give = jnp.einsum("sb,tsn->tbn", orbitals, second, preferred_element_type=f32).astype(bf16)
        whole = join(keep, lax.ppermute(give, "ao", near), 2)
        both = jnp.einsum("tbn,nd->tbd", whole, nu_rows, preferred_element_type=f32)
        here = pick(both, side * side_vir, side_vir, 2)
        there = pick(both, far_side * side_vir, side_vir, 2).astype(bf16)
        dressed.append((here + lax.ppermute(there, "ao", far).astype(f32)).astype(bf16))

    total = jnp.zeros((local_occ, vir, side_vir), f32)
    arrived = []
    for n in range(CHUNKS):
        rows = source_rows[:, n * step:(n + 1) * step]
        sent = jnp.einsum("otc,icd->otid", rows, paired, preferred_element_type=f32).astype(bf16)
        arrived.append(lax.all_to_all(sent, "occ", split_axis=0, concat_axis=0, tiled=True))
    for n in range(CHUNKS):
        both = jnp.einsum("otid,tbd->otib", arrived[n], dressed[n], preferred_element_type=f32)
        here = pick(both, side * side_vir, side_vir, 3)
        there = pick(both, far_side * side_vir, side_vir, 3).astype(bf16)
        summed = (here + lax.ppermute(there, "ao", far).astype(f32)).astype(bf16)
        back = lax.all_to_all(summed, "occ", split_axis=0, concat_axis=0, tiled=True)
        rows = target_rows[:, n * step:(n + 1) * step]
        total = total + jnp.einsum("ota,otib->iab", rows, back, preferred_element_type=f32)
    low, high = total[:, :, :vir_part], total[:, :, vir_part:]
    keep = jnp.where(core == 0, low, high)
    give = jnp.where(core == 0, high, low).astype(bf16)
    return (keep + lax.ppermute(give, "ao", near).astype(f32)).astype(bf16)


def solution(mesh):
    placed = (P("occ", None, "ao"), P(), P("occ", None, "ao"), P(), P(), P(), P())
    return jax.shard_map(
        shards, mesh=mesh, in_specs=placed, out_specs=P("occ", None, "ao"), check_vma=False
    )
```

```python
import functools

import jax
import jax.numpy as jnp
from jax import lax
from jax.experimental import pallas as pl
from jax.experimental.pallas import tpu as pltpu
from jax.sharding import PartitionSpec as P

F32, BF16 = jnp.float32, jnp.bfloat16
TILE_PARTS = 4
VMEM_LIMIT = 50 * 1024 * 1024


def dot(a, b, dims=(((1,), (0,)), ((), ()))):
    return lax.dot_general(a, b, dims, preferred_element_type=F32)


def call(body, outs, ins, flops, scratch=(), early=()):
    whole = pl.BlockSpec(memory_space=pltpu.VMEM)
    moved = sum(2 * x.size for x in ins) + sum(2 * x.size for x in outs)
    return pl.pallas_call(
        body,
        out_shape=outs,
        in_specs=[whole] * len(ins) + [pl.BlockSpec(memory_space=pl.ANY)] * len(early),
        out_specs=[whole] * len(outs),
        scratch_shapes=list(scratch),
        cost_estimate=pl.CostEstimate(flops=flops, bytes_accessed=moved, transcendentals=0),
        compiler_params=pltpu.CompilerParams(vmem_limit_bytes=VMEM_LIMIT),
    )(*ins, *early)


def order_body(orbitals, left, side_rows, held):
    vir = orbitals.shape[1]
    part = lax.axis_index("ao")
    nu_part = side_rows.shape[0] // 2
    line = orbitals[...]
    left[...] = line.T
    quarters = [line[:, q:q + vir // 4] for q in (vir // 4, 0, 3 * vir // 4, vir // 2)]
    line = jnp.where(part % 2 == 0, line, jnp.concatenate(quarters, 1))
    line = jnp.where(part // 2 == 0, line, jnp.concatenate([line[:, vir // 2:], line[:, :vir // 2]], 1))
    held[...] = line
    for q in range(2):
        start = pl.multiple_of((part ^ q) * nu_part, nu_part)
        side_rows[pl.ds(q * nu_part, nu_part), :] = held[pl.ds(start, nu_part), :]


def order_orbitals(orbitals, nu_part):
    count, vir = orbitals.shape
    outs = [jax.ShapeDtypeStruct((vir, count), BF16), jax.ShapeDtypeStruct((2 * nu_part, vir), BF16)]
    return call(order_body, outs, (orbitals,), count * vir, [pltpu.VMEM((count, vir), BF16)])


def gather_body(src, sub, row, count, orbitals, early, source, target, held, ahead, back):
    held[...] = orbitals[...].astype(F32)
    nodes = count.shape[0]
    slots = src.shape[0] // nodes
    half = slots // 2
    blocks = held.shape[0] // nodes
    own, core = lax.axis_index("occ"), lax.axis_index("ao") % 2
    for k in range(nodes):
        partner = own ^ k

        def step(j, carry):
            place = core * half + j
            slot = k * slots + place
            ahead[pl.ds(k * half + j, 1), :] = held[pl.ds(src[slot] * blocks + sub[slot], 1), :]
            line = held[pl.ds(partner * blocks + row[partner * slots + place], 1), :]
            back[pl.ds(k * half + j, 1), :] = jnp.where(place < count[partner], line, 0.0)
            return carry

        lax.fori_loop(0, half, step, 0, unroll=8)
    source[...] = ahead[...].astype(BF16)
    target[...] = back[...].astype(BF16)


def gather_rows(src, sub, row, count, orbitals, early):
    slots, vir = src.shape[0] // 2, orbitals.shape[1]
    scalar = pl.BlockSpec(memory_space=pltpu.SMEM)
    whole = pl.BlockSpec(memory_space=pltpu.VMEM)
    return pl.pallas_call(
        gather_body,
        out_shape=[jax.ShapeDtypeStruct((slots, vir), BF16)] * 2,
        in_specs=[scalar] * 4 + [whole, pl.BlockSpec(memory_space=pl.ANY)],
        out_specs=[whole] * 2,
        scratch_shapes=[pltpu.VMEM(orbitals.shape, F32)] + [pltpu.VMEM((slots, vir), F32)] * 2,
        cost_estimate=pl.CostEstimate(flops=slots * vir, bytes_accessed=8 * slots * vir, transcendentals=0),
        compiler_params=pltpu.CompilerParams(vmem_limit_bytes=VMEM_LIMIT),
    )(src, sub, row, count, orbitals, early)


def rows_body(rows_ref, mine_ref, other_ref, *rest):
    out, scratch = rest[-2:]
    occ = mine_ref.shape[0]
    count, _ = rows_ref.shape
    width = scratch.shape[1]
    rows = rows_ref[...]

    def step(n, carry):
        i = 2 * n
        right = jnp.concatenate([mine_ref[i], other_ref[i], mine_ref[i + 1], other_ref[i + 1]], 0)
        product = dot(rows, right, (((1,), (1,)), ((), ())))
        scratch[pl.ds(i, count, stride=occ), :] = product[:, :width]
        scratch[pl.ds(i + 1, count, stride=occ), :] = product[:, width:]
        return carry

    lax.fori_loop(0, occ // 2, step, 0, unroll=4)
    block = count // out.shape[0] * occ
    for k in range(out.shape[0]):
        out[k] = scratch[k * block:(k + 1) * block, :].reshape(out.shape[1:]).astype(BF16)


def pair_rows(rows, mine, other, nodes, early):
    occ, part, vir = mine.shape
    count = rows.shape[0]
    outs = [jax.ShapeDtypeStruct((nodes, count // nodes, occ, 2 * part), BF16)]
    scratch = [pltpu.VMEM((count * occ, 2 * part), F32)]
    return call(rows_body, outs, (rows, mine, other), 4 * count * occ * vir * part, scratch, early)[0]


def start_copies(other_core, start, tiles, held, sems):
    core = lax.axis_index("ao") % 2
    offset = (1 - core if other_core else core) * (tiles.shape[0] // 2) + start
    pieces = sems.shape[0]
    size = held.shape[0] // pieces
    copies = []
    for n in range(pieces):
        source = tiles.at[pl.ds(offset + n * size, size)]
        copies.append(pltpu.make_async_copy(source, held.at[pl.ds(n * size, size)], sems.at[n]))
        copies[n].start()
    return copies


def pair_dot(left, held, t):
    product = dot(left, jnp.concatenate([held[t], held[t + 1]], 1))
    width = held.shape[2]
    return product[:, :width].astype(BF16), product[:, width:].astype(BF16)


def give_kernel(start, left_ref, tiles, *rest):
    out, held, sems = rest[-3:]
    copies = start_copies(True, start, tiles, held, sems)
    size = out.shape[0] // len(copies)
    left = left_ref[...]
    for n, copy in enumerate(copies):
        copy.wait()
        for t in range(n * size, (n + 1) * size, 2):
            out[t], out[t + 1] = pair_dot(left, held, t)


def finish_kernel(start, skip, left_ref, tiles, other, right_ref, *rest):
    here, there, held, sems = rest[-4:]
    copies = start_copies(False, start, tiles, held, sems)
    size = here.shape[0] // len(copies)
    width = here.shape[1]
    left, right = left_ref[...], right_ref[...]
    side = lax.axis_index("ao") // 2
    for n, copy in enumerate(copies):
        copy.wait()
        rows = []
        for t in range(n * size, (n + 1) * size, 2):
            for j, mine in enumerate(pair_dot(left, held, t)):
                rows.append(jnp.concatenate([mine, other[skip + t + j]], 1))
        both = dot(jnp.concatenate(rows, 0), right).reshape(size, -1, right.shape[1]).astype(BF16)
        piece = pl.ds(n * size, size)
        low, high = both[:, :width], both[:, width:]
        here[piece] = jnp.where(side == 0, low, high)
        away = jnp.where(side == 0, high, low)
        there[piece] = jnp.concatenate([away[:, :, width:], away[:, :, :width]], 2)


PIECE = 4


def tile_call(body, count, tiles, ins, outs, early=()):
    _, sig, nu = tiles.shape
    vir = ins[0].shape[0]
    whole = pl.BlockSpec(memory_space=pltpu.VMEM)
    away = pl.BlockSpec(memory_space=pl.ANY)
    flops = 2 * count * vir * nu * (sig + 2 * vir * (len(outs) - 1))
    return pl.pallas_call(
        body,
        out_shape=outs,
        in_specs=[whole, away] + [whole] * (len(ins) - 1) + [away] * len(early),
        out_specs=[whole] * len(outs),
        scratch_shapes=[pltpu.VMEM((count, sig, nu), BF16), pltpu.SemaphoreType.DMA((count // PIECE,))],
        cost_estimate=pl.CostEstimate(
            flops=flops, bytes_accessed=2 * count * sig * nu * 2, transcendentals=0
        ),
        compiler_params=pltpu.CompilerParams(vmem_limit_bytes=VMEM_LIMIT),
    )(ins[0], tiles, *ins[1:], *early)


def dress_body(parts, *refs):
    out = refs[-1]
    t = 0
    for n in range(parts):
        size = refs[2 * n].shape[0]
        out[t:t + size] = refs[2 * n][...] + refs[2 * n + 1][...]
        t += size


def dress(parts):
    slots = sum(x.shape[0] for x in parts[::2])
    outs = [jax.ShapeDtypeStruct((slots,) + parts[0].shape[1:], BF16)]
    return call(functools.partial(dress_body, len(parts) // 2), outs, parts, slots)[0]


def product_body(near_ref, far_ref, dressed, last, last_far, *refs):
    scratch = refs[-1]
    groups, slots, occ, _ = near_ref.shape
    outs = refs[-1 - groups:-1]
    first = dressed.shape[0]
    for t in range(slots):
        tile = dressed[t] if t < first else last[t - first] + last_far[t - first]
        rows = [jnp.concatenate([near_ref[n, t], far_ref[n, t]], 1) for n in range(groups)]
        product = dot(jnp.concatenate(rows, 0), tile, (((1,), (1,)), ((), ())))
        scratch[pl.ds(t, groups * occ, stride=slots), :] = product
    for n, out in enumerate(outs):
        block = occ * slots
        out[...] = scratch[n * block:(n + 1) * block, :].reshape(out.shape).astype(BF16)


def products(near_rows, far_rows, tiles, early):
    groups, slots, occ, width = near_rows.shape
    outs = [jax.ShapeDtypeStruct((occ, slots, width), BF16)] * groups
    scratch = [pltpu.VMEM((groups * occ * slots, width), F32)]
    flops = 4 * groups * occ * slots * width * width
    return call(product_body, outs, (near_rows, far_rows, *tiles), flops, scratch, early)


def back_body(nodes, rows_ref, *refs):
    values, (keep, give) = refs[:nodes], refs[nodes:]
    occ = values[0].shape[0]
    part = keep.shape[1]
    core = lax.axis_index("ao") % 2
    rows = rows_ref[...]

    def step(i, carry):
        left = jnp.concatenate([v[i] for v in values], 0)
        product = dot(left, rows, (((0,), (0,)), ((), ())))
        low, high = product[:part].astype(BF16), product[part:].astype(BF16)
        keep[i] = jnp.where(core == 0, low, high)
        give[i] = jnp.where(core == 0, high, low)
        return carry

    lax.fori_loop(0, occ, step, 0, unroll=4)


def back_transform(rows, values):
    occ, _, width = values[0].shape
    count, vir = rows.shape
    outs = [jax.ShapeDtypeStruct((occ, width // 2, vir), BF16)] * 2
    return call(
        functools.partial(back_body, len(values)), outs, (rows, *values), 2 * occ * vir * count * width
    )


def shards(amplitudes, orbitals, tiles, tile_count, tile_row, tile_src, tile_sub):
    nodes = lax.axis_size("occ")
    own = lax.axis_index("occ")
    parts = lax.axis_size("ao")
    part = lax.axis_index("ao")
    core = part % 2
    near = [(q, q ^ 1) for q in range(parts)]
    far = [(q, q ^ 2) for q in range(parts)]
    local_occ, vir, vir_part = amplitudes.shape
    nu_part = tiles.shape[2]
    slots = tiles.shape[0]
    half = slots // 2
    blocks = orbitals.shape[0] // nodes
    pick = lax.dynamic_slice_in_dim

    mine = jnp.swapaxes(amplitudes, 1, 2)
    other = lax.ppermute(mine, "ao", near)
    left, side_rows = order_orbitals(orbitals, nu_part)
    def tile_shape(count, width):
        return jax.ShapeDtypeStruct((count, vir, width), BF16)

    def give(start, early):
        outs = [tile_shape(half // 2, nu_part)]
        body = functools.partial(give_kernel, start)
        (given,) = tile_call(body, half // 2, tiles, (left,), outs, early)
        return given, lax.ppermute(given, "ao", near)

    given, first_parts = give(0, ())
    given, second_parts = give(half // 2, [given])
    source_rows, target_rows = gather_rows(tile_src[:, 0], tile_sub, tile_row, tile_count, orbitals, given)
    sent = pair_rows(source_rows, mine, other, nodes, (first_parts, second_parts))
    arrived = lax.all_to_all(sent, "occ", split_axis=0, concat_axis=0, tiled=True)
    parts, early = [], [sent]
    step = half // TILE_PARTS
    for n in range(TILE_PARTS):
        if n >= 2:
            early.append(parts[2 * n - 3])
        other_parts = first_parts if 2 * n < TILE_PARTS else second_parts
        here, there = tile_call(
            functools.partial(finish_kernel, n * step, n * step % (half // 2)), step, tiles,
            (left, other_parts, side_rows), [jax.ShapeDtypeStruct((step, vir // 2, vir), BF16)] * 2, early,
        )
        early = [there]
        parts += [here, lax.ppermute(there, "ao", far)]
    tiles_done = [dress(parts[:-2]), *parts[-2:]]
    units = [[nodes - 1 - n, (n + nodes // 2 - 2) % (nodes // 2)] for n in range(nodes // 2)]
    blocks_of = [jnp.stack([arrived[own ^ k] for k in unit]) for unit in units]
    far_blocks = [lax.ppermute(x, "ao", far) for x in blocks_of]
    returned, early = {}, []
    for n, unit in enumerate(units):
        made = products(blocks_of[n], far_blocks[n], tiles_done, early)
        early = [made[0]]
        if n >= 1:
            early += [returned[k] for k in units[n - 1]]
        for k, x in zip(unit, made):
            returned[k] = lax.ppermute(x, "occ", [(o, o ^ k) for o in range(nodes)]) if k else x
    returned = [returned[k] for k in range(nodes)]
    keep, give_up = back_transform(target_rows, returned)
    return jnp.swapaxes(keep + lax.ppermute(give_up, "ao", near), 1, 2)


def plain_shards(amplitudes, orbitals, tiles, tile_count, tile_row, tile_src, tile_sub):
    nodes = lax.axis_size("occ")
    parts = lax.axis_size("ao")
    part = lax.axis_index("ao")
    core = part % 2
    near = [(q, q ^ 1) for q in range(parts)]
    far = [(q, q ^ 2) for q in range(parts)]
    vir_part = amplitudes.shape[2]
    nu_part = tiles.shape[2]
    slots = tiles.shape[0]
    half = slots // 2
    blocks = orbitals.shape[0] // nodes
    pick = lax.dynamic_slice_in_dim
    ordered = jnp.concatenate([pick(orbitals, (part ^ q) * vir_part, vir_part, 1) for q in range(parts)], 1)
    side_rows = jnp.concatenate([pick(ordered, (part ^ q) * nu_part, nu_part, 0) for q in range(2)], 0)

    def mine_of(table):
        return pick(table.reshape(nodes, slots), core * half, half, 1)

    def product(form, a, b):
        return jnp.einsum(form, a, b, preferred_element_type=F32)

    def split(x, at, axis):
        size = x.shape[axis] // 2
        return pick(x, at * size, size, axis), pick(x, (1 - at) * size, size, axis)

    source = mine_of(tile_src[:, 0]) * blocks + mine_of(tile_sub)
    target = jnp.arange(nodes, dtype=jnp.int32)[:, None] * blocks + mine_of(tile_row)
    place = core * half + jnp.arange(half, dtype=jnp.int32)
    live = place[None, :] < tile_count[:, None]
    source_rows = jnp.take(orbitals, source, axis=0)
    target_rows = jnp.where(live[:, :, None], jnp.take(orbitals, target, axis=0), 0)
    paired = jnp.concatenate([amplitudes, lax.ppermute(amplitudes, "ao", near)], 2)
    sent = product("otc,icd->otid", source_rows, paired).astype(BF16)
    arrived = lax.all_to_all(sent, "occ", split_axis=0, concat_axis=0, tiled=True)
    keep, give = split(product("sb,tsn->tbn", orbitals, tiles).astype(BF16), core, 0)
    whole = jnp.concatenate([keep, lax.ppermute(give, "ao", near)], 2)
    both = product("tbn,nd->tbd", whole, side_rows).astype(BF16)
    dressed = both[:, :, :2 * vir_part] + lax.ppermute(both[:, :, 2 * vir_part:], "ao", far)
    both = product("otid,tbd->otib", arrived, dressed).astype(BF16)
    here, there = split(both, part // 2, 3)
    summed = here + lax.ppermute(there, "ao", far)
    back = lax.all_to_all(summed, "occ", split_axis=0, concat_axis=0, tiled=True)
    total = product("ota,otib->iab", target_rows, back).astype(BF16)
    keep, give = split(total, core, 2)
    return keep + lax.ppermute(give, "ao", near)


def solution(mesh):
    placed = (P("occ", None, "ao"), P(), P("occ", None, "ao"), P(), P(), P(), P())

    def whole(amplitudes, *rest):
        nodes = mesh.shape["occ"]
        rows = amplitudes.shape[0] // nodes
        body = shards if rows % 16 == 0 and nodes <= 16 else plain_shards
        return jax.shard_map(
            body, mesh=mesh, in_specs=placed, out_specs=P("occ", None, "ao"), check_vma=False
        )(amplitudes, *rest)

    return whole
```

```python
import functools

import jax
import jax.numpy as jnp
from jax import lax
from jax.experimental import pallas as pl
from jax.experimental.pallas import tpu as pltpu
from jax.sharding import PartitionSpec as P

F32, BF16 = jnp.float32, jnp.bfloat16
TILE_PARTS = 4
VMEM_LIMIT = 16 * 1024 * 1024
TILE_VMEM_LIMIT = 50 * 1024 * 1024


def dot(a, b, dims=(((1,), (0,)), ((), ()))):
    return lax.dot_general(a, b, dims, preferred_element_type=F32)


def call(body, outs, ins, flops, scratch=(), early=(), limit=VMEM_LIMIT):
    whole = pl.BlockSpec(memory_space=pltpu.VMEM)
    moved = sum(2 * x.size for x in ins) + sum(2 * x.size for x in outs)
    return pl.pallas_call(
        body,
        out_shape=outs,
        in_specs=[whole] * len(ins) + [pl.BlockSpec(memory_space=pl.ANY)] * len(early),
        out_specs=[whole] * len(outs),
        scratch_shapes=list(scratch),
        cost_estimate=pl.CostEstimate(flops=flops, bytes_accessed=moved, transcendentals=0),
        compiler_params=pltpu.CompilerParams(vmem_limit_bytes=limit),
    )(*ins, *early)


def order_body(orbitals, left, side_rows, held):
    vir = orbitals.shape[1]
    part = lax.axis_index("ao")
    nu_part = side_rows.shape[0] // 2
    line = orbitals[...]
    left[...] = line.T
    quarters = [line[:, q:q + vir // 4] for q in (vir // 4, 0, 3 * vir // 4, vir // 2)]
    line = jnp.where(part % 2 == 0, line, jnp.concatenate(quarters, 1))
    line = jnp.where(part // 2 == 0, line, jnp.concatenate([line[:, vir // 2:], line[:, :vir // 2]], 1))
    held[...] = line
    for q in range(2):
        start = pl.multiple_of((part ^ q) * nu_part, nu_part)
        side_rows[pl.ds(q * nu_part, nu_part), :] = held[pl.ds(start, nu_part), :]


def order_orbitals(orbitals, nu_part):
    count, vir = orbitals.shape
    outs = [jax.ShapeDtypeStruct((vir, count), BF16), jax.ShapeDtypeStruct((2 * nu_part, vir), BF16)]
    return call(order_body, outs, (orbitals,), count * vir, [pltpu.VMEM((count, vir), BF16)])


def source_body(src, sub, orbitals, early, source, held, ahead):
    held[...] = orbitals[...].astype(F32)
    nodes = lax.axis_size("occ")
    slots = src.shape[0] // nodes
    half = slots // 2
    blocks = held.shape[0] // nodes
    core = lax.axis_index("ao") % 2
    for k in range(nodes):

        def step(j, carry):
            slot = k * slots + core * half + j
            ahead[pl.ds(k * half + j, 1), :] = held[pl.ds(src[slot] * blocks + sub[slot], 1), :]
            return carry

        lax.fori_loop(0, half, step, 0, unroll=8)
    source[...] = ahead[...].astype(BF16)


def target_body(row, count, orbitals, early, target, held, back):
    held[...] = orbitals[...].astype(F32)
    nodes = count.shape[0]
    slots = row.shape[0] // nodes
    half = slots // 2
    blocks = held.shape[0] // nodes
    own, core = lax.axis_index("occ"), lax.axis_index("ao") % 2
    for k in range(nodes):
        partner = own ^ k

        def step(j, carry):
            place = core * half + j
            line = held[pl.ds(partner * blocks + row[partner * slots + place], 1), :]
            back[pl.ds(k * half + j, 1), :] = jnp.where(place < count[partner], line, 0.0)
            return carry

        lax.fori_loop(0, half, step, 0, unroll=8)
    target[...] = back[...].astype(BF16)


def gather(body, tables, orbitals, early):
    slots, vir = tables[0].shape[0] // 2, orbitals.shape[1]
    scalar = pl.BlockSpec(memory_space=pltpu.SMEM)
    whole = pl.BlockSpec(memory_space=pltpu.VMEM)
    return pl.pallas_call(
        body,
        out_shape=jax.ShapeDtypeStruct((slots, vir), BF16),
        in_specs=[scalar] * 2 + [whole, pl.BlockSpec(memory_space=pl.ANY)],
        out_specs=whole,
        scratch_shapes=[pltpu.VMEM(orbitals.shape, F32), pltpu.VMEM((slots, vir), F32)],
        cost_estimate=pl.CostEstimate(flops=slots * vir, bytes_accessed=4 * slots * vir, transcendentals=0),
        compiler_params=pltpu.CompilerParams(vmem_limit_bytes=VMEM_LIMIT),
    )(*tables, orbitals, early)


def rows_body(rows_ref, mine_ref, other_ref, *rest):
    out = rest[-1]
    nodes, occ, slots, width = out.shape
    rows = rows_ref[...]

    def step(n, carry):
        i = 2 * n
        right = jnp.concatenate([mine_ref[i], other_ref[i], mine_ref[i + 1], other_ref[i + 1]], 0)
        product = dot(rows, right, (((1,), (1,)), ((), ()))).astype(BF16)
        for j in range(2):
            out[:, i + j] = product[:, j * width:(j + 1) * width].reshape(nodes, slots, width)
        return carry

    lax.fori_loop(0, occ // 2, step, 0, unroll=4)


def pair_rows(rows, mine, other, nodes, early):
    occ, part, vir = mine.shape
    count = rows.shape[0]
    outs = [jax.ShapeDtypeStruct((nodes, occ, count // nodes, 2 * part), BF16)]
    return call(rows_body, outs, (rows, mine, other), 4 * count * occ * vir * part, (), early, TILE_VMEM_LIMIT)[0]


def turn_body(groups, meta, *refs):
    blocks, (out, held) = refs[:groups], refs[-2:]
    _, occ, slots, width = blocks[0].shape
    for n in range(groups):
        base = n * occ * slots
        held[base:base + occ * slots, :] = blocks[n][0].astype(F32).reshape(occ * slots, width)
        for t in range(slots):
            out[n, t] = held[pl.ds(base + t, occ, stride=slots), :].astype(BF16)


def turn(own, arrived, partners, early):
    groups = len(partners)
    _, occ, slots, width = arrived.shape
    specs = [
        pl.BlockSpec((1, occ, slots, width), lambda n, ref, k=k: (ref[0] ^ k, 0, 0, 0)) for k in partners
    ]
    return pl.pallas_call(
        functools.partial(turn_body, groups),
        out_shape=jax.ShapeDtypeStruct((groups, slots, occ, width), BF16),
        grid_spec=pltpu.PrefetchScalarGridSpec(
            num_scalar_prefetch=1,
            grid=(1,),
            in_specs=specs + [pl.BlockSpec(memory_space=pl.ANY)] * len(early),
            out_specs=pl.BlockSpec(memory_space=pltpu.VMEM),
            scratch_shapes=[pltpu.VMEM((groups * occ * slots, width), F32)],
        ),
        cost_estimate=pl.CostEstimate(
            flops=groups * occ * slots * width, bytes_accessed=4 * groups * occ * slots * width, transcendentals=0
        ),
        compiler_params=pltpu.CompilerParams(vmem_limit_bytes=VMEM_LIMIT),
    )(jnp.reshape(own, (1,)), *[arrived] * groups, *early)


def start_copies(other_core, start, tiles, held, sems):
    core = lax.axis_index("ao") % 2
    offset = (1 - core if other_core else core) * (tiles.shape[0] // 2) + start
    pieces = sems.shape[0]
    size = held.shape[0] // pieces
    copies = []
    for n in range(pieces):
        source = tiles.at[pl.ds(offset + n * size, size)]
        copies.append(pltpu.make_async_copy(source, held.at[pl.ds(n * size, size)], sems.at[n]))
        copies[n].start()
    return copies


def pair_dot(left, held, t):
    product = dot(left, jnp.concatenate([held[t], held[t + 1]], 1))
    width = held.shape[2]
    return product[:, :width].astype(BF16), product[:, width:].astype(BF16)


def give_kernel(start, left_ref, tiles, *rest):
    out, held, sems = rest[-3:]
    copies = start_copies(True, start, tiles, held, sems)
    size = out.shape[0] // len(copies)
    left = left_ref[...]
    for n, copy in enumerate(copies):
        copy.wait()
        for t in range(n * size, (n + 1) * size, 2):
            out[t], out[t + 1] = pair_dot(left, held, t)


def finish_kernel(start, skip, left_ref, tiles, other, right_ref, *rest):
    here, there, held, sems = rest[-4:]
    copies = start_copies(False, start, tiles, held, sems)
    size = here.shape[0] // len(copies)
    width = here.shape[1]
    left, right = left_ref[...], right_ref[...]
    side = lax.axis_index("ao") // 2
    for n, copy in enumerate(copies):
        copy.wait()
        rows = []
        for t in range(n * size, (n + 1) * size, 2):
            for j, mine in enumerate(pair_dot(left, held, t)):
                rows.append(jnp.concatenate([mine, other[skip + t + j]], 1))
        both = dot(jnp.concatenate(rows, 0), right).reshape(size, -1, right.shape[1]).astype(BF16)
        piece = pl.ds(n * size, size)
        low, high = both[:, :width], both[:, width:]
        here[piece] = jnp.where(side == 0, low, high)
        away = jnp.where(side == 0, high, low)
        there[piece] = jnp.concatenate([away[:, :, width:], away[:, :, :width]], 2)


PIECE = 4


def tile_call(body, count, tiles, ins, outs, early=()):
    _, sig, nu = tiles.shape
    vir = ins[0].shape[0]
    whole = pl.BlockSpec(memory_space=pltpu.VMEM)
    away = pl.BlockSpec(memory_space=pl.ANY)
    flops = 2 * count * vir * nu * (sig + 2 * vir * (len(outs) - 1))
    return pl.pallas_call(
        body,
        out_shape=outs,
        in_specs=[whole, away] + [whole] * (len(ins) - 1) + [away] * len(early),
        out_specs=[whole] * len(outs),
        scratch_shapes=[pltpu.VMEM((count, sig, nu), BF16), pltpu.SemaphoreType.DMA((count // PIECE,))],
        cost_estimate=pl.CostEstimate(
            flops=flops, bytes_accessed=2 * count * sig * nu * 2, transcendentals=0
        ),
        compiler_params=pltpu.CompilerParams(vmem_limit_bytes=TILE_VMEM_LIMIT),
    )(ins[0], tiles, *ins[1:], *early)


def dress_body(parts, *refs):
    out = refs[-1]
    t = 0
    for n in range(parts):
        size = refs[2 * n].shape[0]
        out[t:t + size] = refs[2 * n][...] + refs[2 * n + 1][...]
        t += size


def dress(parts):
    slots = sum(x.shape[0] for x in parts[::2])
    outs = [jax.ShapeDtypeStruct((slots,) + parts[0].shape[1:], BF16)]
    return call(functools.partial(dress_body, len(parts) // 2), outs, parts, slots)[0]


def product_body(near_ref, far_ref, dressed, last, last_far, *refs):
    scratch = refs[-1]
    groups, slots, occ, _ = near_ref.shape
    outs = refs[-1 - groups:-1]
    first = dressed.shape[0]
    for t in range(slots):
        tile = dressed[t] if t < first else last[t - first] + last_far[t - first]
        rows = [jnp.concatenate([near_ref[n, t], far_ref[n, t]], 1) for n in range(groups)]
        product = dot(jnp.concatenate(rows, 0), tile, (((1,), (1,)), ((), ())))
        scratch[pl.ds(t, groups * occ, stride=slots), :] = product
    for n, out in enumerate(outs):
        block = occ * slots
        out[...] = scratch[n * block:(n + 1) * block, :].reshape(out.shape).astype(BF16)


def products(near_rows, far_rows, tiles, early):
    groups, slots, occ, width = near_rows.shape
    outs = [jax.ShapeDtypeStruct((occ, slots, width), BF16)] * groups
    scratch = [pltpu.VMEM((groups * occ * slots, width), F32)]
    flops = 4 * groups * occ * slots * width * width
    return call(product_body, outs, (near_rows, far_rows, *tiles), flops, scratch, early)


def copy_body(rows, *rest):
    rest[-1][...] = rows[...]


def rows_after(rows, early):
    return call(copy_body, [jax.ShapeDtypeStruct(rows.shape, BF16)], (rows,), rows.size, (), early)[0]


def back_body(nodes, rows_ref, *refs):
    values, (keep, give) = refs[:nodes], refs[nodes:]
    occ = values[0].shape[0]
    part = keep.shape[1]
    core = lax.axis_index("ao") % 2
    rows = rows_ref[...]

    def step(i, carry):
        left = jnp.concatenate([v[i] for v in values], 0)
        product = dot(left, rows, (((0,), (0,)), ((), ())))
        low, high = product[:part].astype(BF16), product[part:].astype(BF16)
        keep[i] = jnp.where(core == 0, low, high)
        give[i] = jnp.where(core == 0, high, low)
        return carry

    lax.fori_loop(0, occ, step, 0, unroll=4)


def back_transform(rows, values):
    occ, _, width = values[0].shape
    count, vir = rows.shape
    outs = [jax.ShapeDtypeStruct((occ, width // 2, vir), BF16)] * 2
    return call(
        functools.partial(back_body, len(values)), outs, (rows, *values), 2 * occ * vir * count * width
    )


def shards(amplitudes, orbitals, tiles, tile_count, tile_row, tile_src, tile_sub):
    nodes = lax.axis_size("occ")
    own = lax.axis_index("occ")
    parts = lax.axis_size("ao")
    part = lax.axis_index("ao")
    core = part % 2
    near = [(q, q ^ 1) for q in range(parts)]
    far = [(q, q ^ 2) for q in range(parts)]
    local_occ, vir, vir_part = amplitudes.shape
    nu_part = tiles.shape[2]
    slots = tiles.shape[0]
    half = slots // 2
    blocks = orbitals.shape[0] // nodes
    pick = lax.dynamic_slice_in_dim

    mine = jnp.swapaxes(amplitudes, 1, 2)
    other = lax.ppermute(mine, "ao", near)
    left, side_rows = order_orbitals(orbitals, nu_part)
    def tile_shape(count, width):
        return jax.ShapeDtypeStruct((count, vir, width), BF16)

    def give(start, early):
        outs = [tile_shape(half // 2, nu_part)]
        body = functools.partial(give_kernel, start)
        (given,) = tile_call(body, half // 2, tiles, (left,), outs, early)
        return given, lax.ppermute(given, "ao", near)

    given, first_parts = give(0, ())
    given, second_parts = give(half // 2, [given])
    source_rows = gather(source_body, (tile_src[:, 0], tile_sub), orbitals, given)
    sent = pair_rows(source_rows, mine, other, nodes, (first_parts, second_parts))
    arrived = lax.all_to_all(sent, "occ", split_axis=0, concat_axis=0, tiled=True)
    parts, early = [], [sent]
    step = half // TILE_PARTS
    for n in range(TILE_PARTS):
        if n >= 2:
            early.append(parts[2 * n - 3])
        other_parts = first_parts if 2 * n < TILE_PARTS else second_parts
        here, there = tile_call(
            functools.partial(finish_kernel, n * step, n * step % (half // 2)), step, tiles,
            (left, other_parts, side_rows), [jax.ShapeDtypeStruct((step, vir // 2, vir), BF16)] * 2, early,
        )
        early = [there]
        parts += [here, lax.ppermute(there, "ao", far)]
    target_rows = gather(target_body, (tile_row, tile_count), orbitals, early[0])
    tiles_done = [dress(parts[:-2]), *parts[-2:]]
    units = [[nodes - 1 - n, (n + nodes // 2 - 2) % (nodes // 2)] for n in range(nodes // 2)]
    wait_for = {2: (0,), 3: (1,)}
    blocks_of, far_blocks = [], []
    for unit in units:
        blocks_of.append(turn(own, arrived, unit, blocks_of[-1:]))
        far_blocks.append(lax.ppermute(blocks_of[-1], "ao", far))
    returned, early = {}, []
    for n, unit in enumerate(units):
        made = products(blocks_of[n], far_blocks[n], tiles_done, early)
        early = [made[0]]
        for m in wait_for.get(n, ()):
            early += [returned[k] for k in units[m]]
        for k, x in zip(unit, made):
            returned[k] = lax.ppermute(x, "occ", [(o, o ^ k) for o in range(nodes)]) if k else x
    tied = [returned[k] for m in (2,) for k in units[m]]
    target_rows = rows_after(target_rows, tied)
    returned = [returned[k] for k in range(nodes)]
    keep, give_up = back_transform(target_rows, returned)
    return jnp.swapaxes(keep + lax.ppermute(give_up, "ao", near), 1, 2)


def plain_shards(amplitudes, orbitals, tiles, tile_count, tile_row, tile_src, tile_sub):
    nodes = lax.axis_size("occ")
    parts = lax.axis_size("ao")
    part = lax.axis_index("ao")
    core = part % 2
    near = [(q, q ^ 1) for q in range(parts)]
    far = [(q, q ^ 2) for q in range(parts)]
    vir_part = amplitudes.shape[2]
    nu_part = tiles.shape[2]
    slots = tiles.shape[0]
    half = slots // 2
    blocks = orbitals.shape[0] // nodes
    pick = lax.dynamic_slice_in_dim
    ordered = jnp.concatenate([pick(orbitals, (part ^ q) * vir_part, vir_part, 1) for q in range(parts)], 1)
    side_rows = jnp.concatenate([pick(ordered, (part ^ q) * nu_part, nu_part, 0) for q in range(2)], 0)

    def mine_of(table):
        return pick(table.reshape(nodes, slots), core * half, half, 1)

    def product(form, a, b):
        return jnp.einsum(form, a, b, preferred_element_type=F32)

    def split(x, at, axis):
        size = x.shape[axis] // 2
        return pick(x, at * size, size, axis), pick(x, (1 - at) * size, size, axis)

    source = mine_of(tile_src[:, 0]) * blocks + mine_of(tile_sub)
    target = jnp.arange(nodes, dtype=jnp.int32)[:, None] * blocks + mine_of(tile_row)
    place = core * half + jnp.arange(half, dtype=jnp.int32)
    live = place[None, :] < tile_count[:, None]
    source_rows = jnp.take(orbitals, source, axis=0)
    target_rows = jnp.where(live[:, :, None], jnp.take(orbitals, target, axis=0), 0)
    paired = jnp.concatenate([amplitudes, lax.ppermute(amplitudes, "ao", near)], 2)
    sent = product("otc,icd->otid", source_rows, paired).astype(BF16)
    arrived = lax.all_to_all(sent, "occ", split_axis=0, concat_axis=0, tiled=True)
    keep, give = split(product("sb,tsn->tbn", orbitals, tiles).astype(BF16), core, 0)
    whole = jnp.concatenate([keep, lax.ppermute(give, "ao", near)], 2)
    both = product("tbn,nd->tbd", whole, side_rows).astype(BF16)
    dressed = both[:, :, :2 * vir_part] + lax.ppermute(both[:, :, 2 * vir_part:], "ao", far)
    both = product("otid,tbd->otib", arrived, dressed).astype(BF16)
    here, there = split(both, part // 2, 3)
    summed = here + lax.ppermute(there, "ao", far)
    back = lax.all_to_all(summed, "occ", split_axis=0, concat_axis=0, tiled=True)
    total = product("ota,otib->iab", target_rows, back).astype(BF16)
    keep, give = split(total, core, 2)
    return keep + lax.ppermute(give, "ao", near)


def solution(mesh):
    placed = (P("occ", None, "ao"), P(), P("occ", None, "ao"), P(), P(), P(), P())

    def whole(amplitudes, *rest):
        nodes = mesh.shape["occ"]
        rows = amplitudes.shape[0] // nodes
        body = shards if rows % 16 == 0 and nodes <= 16 else plain_shards
        return jax.shard_map(
            body, mesh=mesh, in_specs=placed, out_specs=P("occ", None, "ao"), check_vma=False
        )(amplitudes, *rest)

    return whole
```

```python
import functools

import jax
import jax.numpy as jnp
from jax import lax
from jax.experimental import pallas as pl
from jax.experimental.pallas import tpu as pltpu
from jax.sharding import PartitionSpec as P

F32, BF16 = jnp.float32, jnp.bfloat16
TILE_PARTS = 4
VMEM_LIMIT = 16 * 1024 * 1024
TILE_VMEM_LIMIT = 50 * 1024 * 1024


def dot(a, b, dims=(((1,), (0,)), ((), ()))):
    return lax.dot_general(a, b, dims, preferred_element_type=F32)


def call(body, outs, ins, flops, scratch=(), early=(), limit=VMEM_LIMIT):
    whole = pl.BlockSpec(memory_space=pltpu.VMEM)
    moved = sum(2 * x.size for x in ins) + sum(2 * x.size for x in outs)
    return pl.pallas_call(
        body,
        out_shape=outs,
        in_specs=[whole] * len(ins) + [pl.BlockSpec(memory_space=pl.ANY)] * len(early),
        out_specs=[whole] * len(outs),
        scratch_shapes=list(scratch),
        cost_estimate=pl.CostEstimate(flops=flops, bytes_accessed=moved, transcendentals=0),
        compiler_params=pltpu.CompilerParams(vmem_limit_bytes=limit),
    )(*ins, *early)


def order_body(orbitals, left, side_rows, held):
    vir = orbitals.shape[1]
    part = lax.axis_index("ao")
    nu_part = side_rows.shape[0] // 2
    line = orbitals[...]
    left[...] = line.T
    quarters = [line[:, q:q + vir // 4] for q in (vir // 4, 0, 3 * vir // 4, vir // 2)]
    line = jnp.where(part % 2 == 0, line, jnp.concatenate(quarters, 1))
    line = jnp.where(part // 2 == 0, line, jnp.concatenate([line[:, vir // 2:], line[:, :vir // 2]], 1))
    held[...] = line
    for q in range(2):
        start = pl.multiple_of((part ^ q) * nu_part, nu_part)
        side_rows[pl.ds(q * nu_part, nu_part), :] = held[pl.ds(start, nu_part), :]


def order_orbitals(orbitals, nu_part):
    count, vir = orbitals.shape
    outs = [jax.ShapeDtypeStruct((vir, count), BF16), jax.ShapeDtypeStruct((2 * nu_part, vir), BF16)]
    return call(order_body, outs, (orbitals,), count * vir, [pltpu.VMEM((count, vir), BF16)])


def source_body(src, sub, orbitals, early, source, held, ahead):
    held[...] = orbitals[...].astype(F32)
    nodes = lax.axis_size("occ")
    slots = src.shape[0] // nodes
    half = slots // 2
    blocks = held.shape[0] // nodes
    core = lax.axis_index("ao") % 2
    for k in range(nodes):

        def step(j, carry):
            slot = k * slots + core * half + j
            ahead[pl.ds(k * half + j, 1), :] = held[pl.ds(src[slot] * blocks + sub[slot], 1), :]
            return carry

        lax.fori_loop(0, half, step, 0, unroll=8)
    source[...] = ahead[...].astype(BF16)


def target_body(row, count, orbitals, early, target, held, back):
    held[...] = orbitals[...].astype(F32)
    nodes = count.shape[0]
    slots = row.shape[0] // nodes
    half = slots // 2
    blocks = held.shape[0] // nodes
    own, core = lax.axis_index("occ"), lax.axis_index("ao") % 2
    for k in range(nodes):
        partner = own ^ k

        def step(j, carry):
            place = core * half + j
            line = held[pl.ds(partner * blocks + row[partner * slots + place], 1), :]
            back[pl.ds(k * half + j, 1), :] = jnp.where(place < count[partner], line, 0.0)
            return carry

        lax.fori_loop(0, half, step, 0, unroll=8)
    target[...] = back[...].astype(BF16)


def gather(body, tables, orbitals, early):
    slots, vir = tables[0].shape[0] // 2, orbitals.shape[1]
    scalar = pl.BlockSpec(memory_space=pltpu.SMEM)
    whole = pl.BlockSpec(memory_space=pltpu.VMEM)
    return pl.pallas_call(
        body,
        out_shape=jax.ShapeDtypeStruct((slots, vir), BF16),
        in_specs=[scalar] * 2 + [whole, pl.BlockSpec(memory_space=pl.ANY)],
        out_specs=whole,
        scratch_shapes=[pltpu.VMEM(orbitals.shape, F32), pltpu.VMEM((slots, vir), F32)],
        cost_estimate=pl.CostEstimate(flops=slots * vir, bytes_accessed=4 * slots * vir, transcendentals=0),
        compiler_params=pltpu.CompilerParams(vmem_limit_bytes=VMEM_LIMIT),
    )(*tables, orbitals, early)


def rows_body(rows_ref, mine_ref, other_ref, *rest):
    out, held, sems = rest[-3:]
    nodes, occ, slots, width = held.shape
    rows = rows_ref[...]
    copies = []
    part = occ // sems.shape[0]
    for s in range(sems.shape[0]):
        for i in range(s * part, (s + 1) * part, 2):
            right = jnp.concatenate([mine_ref[i], other_ref[i], mine_ref[i + 1], other_ref[i + 1]], 0)
            product = dot(rows, right, (((1,), (1,)), ((), ()))).astype(BF16)
            for j in range(2):
                held[:, i + j] = product[:, j * width:(j + 1) * width].reshape(nodes, slots, width)
        piece = pl.ds(s * part, part)
        copies.append(pltpu.make_async_copy(held.at[:, piece], out.at[:, piece], sems.at[s]))
        copies[-1].start()
    for copy in copies:
        copy.wait()


def pair_rows(rows, mine, other, nodes, early):
    occ, part, vir = mine.shape
    count = rows.shape[0]
    shape = (nodes, occ, count // nodes, 2 * part)
    whole = pl.BlockSpec(memory_space=pltpu.VMEM)
    away = pl.BlockSpec(memory_space=pl.ANY)
    return pl.pallas_call(
        rows_body,
        out_shape=jax.ShapeDtypeStruct(shape, BF16),
        in_specs=[whole] * 3 + [away] * len(early),
        out_specs=pl.BlockSpec(memory_space=pltpu.HBM),
        scratch_shapes=[pltpu.VMEM(shape, BF16), pltpu.SemaphoreType.DMA((4,))],
        cost_estimate=pl.CostEstimate(
            flops=4 * count * occ * vir * part, bytes_accessed=4 * occ * part * vir, transcendentals=0
        ),
        compiler_params=pltpu.CompilerParams(vmem_limit_bytes=TILE_VMEM_LIMIT),
    )(rows, mine, other, *early)


def turn_body(groups, meta, *refs):
    blocks, (out, held) = refs[:groups], refs[-2:]
    _, occ, slots, width = blocks[0].shape
    for n in range(groups):
        base = n * occ * slots
        held[base:base + occ * slots, :] = blocks[n][0].astype(F32).reshape(occ * slots, width)
        for t in range(slots):
            out[n, t] = held[pl.ds(base + t, occ, stride=slots), :].astype(BF16)


def turn(own, arrived, partners, early):
    groups = len(partners)
    _, occ, slots, width = arrived.shape
    specs = [
        pl.BlockSpec((1, occ, slots, width), lambda n, ref, k=k: (ref[0] ^ k, 0, 0, 0)) for k in partners
    ]
    return pl.pallas_call(
        functools.partial(turn_body, groups),
        out_shape=jax.ShapeDtypeStruct((groups, slots, occ, width), BF16),
        grid_spec=pltpu.PrefetchScalarGridSpec(
            num_scalar_prefetch=1,
            grid=(1,),
            in_specs=specs + [pl.BlockSpec(memory_space=pl.ANY)] * len(early),
            out_specs=pl.BlockSpec(memory_space=pltpu.VMEM),
            scratch_shapes=[pltpu.VMEM((groups * occ * slots, width), F32)],
        ),
        cost_estimate=pl.CostEstimate(
            flops=groups * occ * slots * width, bytes_accessed=4 * groups * occ * slots * width, transcendentals=0
        ),
        compiler_params=pltpu.CompilerParams(vmem_limit_bytes=VMEM_LIMIT),
    )(jnp.reshape(own, (1,)), *[arrived] * groups, *early)


def start_copies(other_core, start, tiles, held, sems):
    core = lax.axis_index("ao") % 2
    offset = (1 - core if other_core else core) * (tiles.shape[0] // 2) + start
    pieces = sems.shape[0]
    size = held.shape[0] // pieces
    copies = []
    for n in range(pieces):
        source = tiles.at[pl.ds(offset + n * size, size)]
        copies.append(pltpu.make_async_copy(source, held.at[pl.ds(n * size, size)], sems.at[n]))
        copies[n].start()
    return copies


def pair_dot(left, held, t):
    product = dot(left, jnp.concatenate([held[t], held[t + 1]], 1))
    width = held.shape[2]
    return product[:, :width].astype(BF16), product[:, width:].astype(BF16)


def give_kernel(start, left_ref, tiles, *rest):
    out, held, sems = rest[-3:]
    copies = start_copies(True, start, tiles, held, sems)
    size = out.shape[0] // len(copies)
    left = left_ref[...]
    for n, copy in enumerate(copies):
        copy.wait()
        for t in range(n * size, (n + 1) * size, 2):
            out[t], out[t + 1] = pair_dot(left, held, t)


def finish_kernel(start, skip, left_ref, tiles, other, right_ref, *rest):
    here, there, held, sems = rest[-4:]
    copies = start_copies(False, start, tiles, held, sems)
    size = here.shape[0] // len(copies)
    width = here.shape[1]
    left, right = left_ref[...], right_ref[...]
    side = lax.axis_index("ao") // 2
    for n, copy in enumerate(copies):
        copy.wait()
        rows = []
        for t in range(n * size, (n + 1) * size, 2):
            for j, mine in enumerate(pair_dot(left, held, t)):
                rows.append(jnp.concatenate([mine, other[skip + t + j]], 1))
        both = dot(jnp.concatenate(rows, 0), right).reshape(size, -1, right.shape[1]).astype(BF16)
        piece = pl.ds(n * size, size)
        low, high = both[:, :width], both[:, width:]
        here[piece] = jnp.where(side == 0, low, high)
        away = jnp.where(side == 0, high, low)
        there[piece] = jnp.concatenate([away[:, :, width:], away[:, :, :width]], 2)


PIECE = 4


def tile_call(body, count, tiles, ins, outs, early=()):
    _, sig, nu = tiles.shape
    vir = ins[0].shape[0]
    whole = pl.BlockSpec(memory_space=pltpu.VMEM)
    away = pl.BlockSpec(memory_space=pl.ANY)
    flops = 2 * count * vir * nu * (sig + 2 * vir * (len(outs) - 1))
    return pl.pallas_call(
        body,
        out_shape=outs,
        in_specs=[whole, away] + [whole] * (len(ins) - 1) + [away] * len(early),
        out_specs=[whole] * len(outs),
        scratch_shapes=[pltpu.VMEM((count, sig, nu), BF16), pltpu.SemaphoreType.DMA((count // PIECE,))],
        cost_estimate=pl.CostEstimate(
            flops=flops, bytes_accessed=2 * count * sig * nu * 2, transcendentals=0
        ),
        compiler_params=pltpu.CompilerParams(vmem_limit_bytes=TILE_VMEM_LIMIT),
    )(ins[0], tiles, *ins[1:], *early)


def dress_body(parts, *refs):
    out = refs[-1]
    t = 0
    for n in range(parts):
        size = refs[2 * n].shape[0]
        out[t:t + size] = refs[2 * n][...] + refs[2 * n + 1][...]
        t += size


def dress(parts):
    slots = sum(x.shape[0] for x in parts[::2])
    outs = [jax.ShapeDtypeStruct((slots,) + parts[0].shape[1:], BF16)]
    return call(functools.partial(dress_body, len(parts) // 2), outs, parts, slots)[0]


def product_body(near_ref, far_ref, dressed, last, last_far, *refs):
    scratch = refs[-1]
    groups, slots, occ, _ = near_ref.shape
    outs = refs[-1 - groups:-1]
    first = dressed.shape[0]
    for t in range(slots):
        tile = dressed[t] if t < first else last[t - first] + last_far[t - first]
        rows = [jnp.concatenate([near_ref[n, t], far_ref[n, t]], 1) for n in range(groups)]
        product = dot(jnp.concatenate(rows, 0), tile, (((1,), (1,)), ((), ())))
        scratch[pl.ds(t, groups * occ, stride=slots), :] = product
    for n, out in enumerate(outs):
        block = occ * slots
        out[...] = scratch[n * block:(n + 1) * block, :].reshape(out.shape).astype(BF16)


def products(near_rows, far_rows, tiles, early):
    groups, slots, occ, width = near_rows.shape
    outs = [jax.ShapeDtypeStruct((occ, slots, width), BF16)] * groups
    scratch = [pltpu.VMEM((groups * occ * slots, width), F32)]
    flops = 4 * groups * occ * slots * width * width
    return call(product_body, outs, (near_rows, far_rows, *tiles), flops, scratch, early)


def copy_body(rows, *rest):
    rest[-1][...] = rows[...]


def rows_after(rows, early):
    return call(copy_body, [jax.ShapeDtypeStruct(rows.shape, BF16)], (rows,), rows.size, (), early)[0]


def back_body(nodes, rows_ref, *refs):
    values, (keep, give) = refs[:nodes], refs[nodes:]
    occ = values[0].shape[0]
    part = keep.shape[1]
    core = lax.axis_index("ao") % 2
    rows = rows_ref[...]

    def step(i, carry):
        left = jnp.concatenate([v[i] for v in values], 0)
        product = dot(left, rows, (((0,), (0,)), ((), ())))
        low, high = product[:part].astype(BF16), product[part:].astype(BF16)
        keep[i] = jnp.where(core == 0, low, high)
        give[i] = jnp.where(core == 0, high, low)
        return carry

    lax.fori_loop(0, occ, step, 0, unroll=4)


def back_transform(rows, values):
    occ, _, width = values[0].shape
    count, vir = rows.shape
    outs = [jax.ShapeDtypeStruct((occ, width // 2, vir), BF16)] * 2
    return call(
        functools.partial(back_body, len(values)), outs, (rows, *values), 2 * occ * vir * count * width
    )


def shards(amplitudes, orbitals, tiles, tile_count, tile_row, tile_src, tile_sub):
    nodes = lax.axis_size("occ")
    own = lax.axis_index("occ")
    parts = lax.axis_size("ao")
    part = lax.axis_index("ao")
    core = part % 2
    near = [(q, q ^ 1) for q in range(parts)]
    far = [(q, q ^ 2) for q in range(parts)]
    local_occ, vir, vir_part = amplitudes.shape
    nu_part = tiles.shape[2]
    slots = tiles.shape[0]
    half = slots // 2
    blocks = orbitals.shape[0] // nodes
    pick = lax.dynamic_slice_in_dim

    mine = jnp.swapaxes(amplitudes, 1, 2)
    other = lax.ppermute(mine, "ao", near)
    left, side_rows = order_orbitals(orbitals, nu_part)
    def tile_shape(count, width):
        return jax.ShapeDtypeStruct((count, vir, width), BF16)

    def give(start, early):
        outs = [tile_shape(half // 2, nu_part)]
        body = functools.partial(give_kernel, start)
        (given,) = tile_call(body, half // 2, tiles, (left,), outs, early)
        return given, lax.ppermute(given, "ao", near)

    given, first_parts = give(0, ())
    given, second_parts = give(half // 2, [given, other])
    source_rows = gather(source_body, (tile_src[:, 0], tile_sub), orbitals, given)
    sent = pair_rows(source_rows, mine, other, nodes, (first_parts, second_parts))
    arrived = lax.all_to_all(sent, "occ", split_axis=0, concat_axis=0, tiled=True)
    parts, early = [], [sent]
    step = half // TILE_PARTS
    for n in range(TILE_PARTS):
        if n >= 2:
            early.append(parts[2 * n - 3])
        other_parts = first_parts if 2 * n < TILE_PARTS else second_parts
        here, there = tile_call(
            functools.partial(finish_kernel, n * step, n * step % (half // 2)), step, tiles,
            (left, other_parts, side_rows), [jax.ShapeDtypeStruct((step, vir // 2, vir), BF16)] * 2, early,
        )
        early = [there]
        parts += [here, lax.ppermute(there, "ao", far)]
    target_rows = gather(target_body, (tile_row, tile_count), orbitals, early[0])
    tiles_done = [dress(parts[:-2]), *parts[-2:]]
    lower = nodes // 2
    light = [k for k in ((n + lower // 2) % lower for n in range(lower)) if k] + [0]
    units = [[nodes - 1]]
    for n in range(1, lower):
        units += [[nodes - 1 - n], [light[n - 1]]]
    units.append([light[-1]])
    wait_for = {4: (0,), 5: (1,), 6: (2, 3), 7: (4,)}
    blocks_of, far_blocks = [], []
    for unit in units:
        blocks_of.append(turn(own, arrived, unit, blocks_of[-1:]))
        far_blocks.append(lax.ppermute(blocks_of[-1], "ao", far))
    returned, made = {}, []
    for n, unit in enumerate(units):
        early = list(made[:1]) + [returned[k] for m in wait_for.get(n, ()) for k in units[m]]
        made = products(blocks_of[n], far_blocks[n], tiles_done, early)
        for k, x in zip(unit, made):
            returned[k] = lax.ppermute(x, "occ", [(o, o ^ k) for o in range(nodes)]) if k else x
    last_far = [returned[k] for k in (lower, lower + 1)]
    target_rows = rows_after(target_rows, last_far[:1])
    returned = [returned[k] for k in range(nodes)]
    keep, give_up = back_transform(target_rows, returned)
    return jnp.swapaxes(keep + lax.ppermute(give_up, "ao", near), 1, 2)


def plain_shards(amplitudes, orbitals, tiles, tile_count, tile_row, tile_src, tile_sub):
    nodes = lax.axis_size("occ")
    parts = lax.axis_size("ao")
    part = lax.axis_index("ao")
    core = part % 2
    near = [(q, q ^ 1) for q in range(parts)]
    far = [(q, q ^ 2) for q in range(parts)]
    vir_part = amplitudes.shape[2]
    nu_part = tiles.shape[2]
    slots = tiles.shape[0]
    half = slots // 2
    blocks = orbitals.shape[0] // nodes
    pick = lax.dynamic_slice_in_dim
    ordered = jnp.concatenate([pick(orbitals, (part ^ q) * vir_part, vir_part, 1) for q in range(parts)], 1)
    side_rows = jnp.concatenate([pick(ordered, (part ^ q) * nu_part, nu_part, 0) for q in range(2)], 0)

    def mine_of(table):
        return pick(table.reshape(nodes, slots), core * half, half, 1)

    def product(form, a, b):
        return jnp.einsum(form, a, b, preferred_element_type=F32)

    def split(x, at, axis):
        size = x.shape[axis] // 2
        return pick(x, at * size, size, axis), pick(x, (1 - at) * size, size, axis)

    source = mine_of(tile_src[:, 0]) * blocks + mine_of(tile_sub)
    target = jnp.arange(nodes, dtype=jnp.int32)[:, None] * blocks + mine_of(tile_row)
    place = core * half + jnp.arange(half, dtype=jnp.int32)
    live = place[None, :] < tile_count[:, None]
    source_rows = jnp.take(orbitals, source, axis=0)
    target_rows = jnp.where(live[:, :, None], jnp.take(orbitals, target, axis=0), 0)
    paired = jnp.concatenate([amplitudes, lax.ppermute(amplitudes, "ao", near)], 2)
    sent = product("otc,icd->otid", source_rows, paired).astype(BF16)
    arrived = lax.all_to_all(sent, "occ", split_axis=0, concat_axis=0, tiled=True)
    keep, give = split(product("sb,tsn->tbn", orbitals, tiles).astype(BF16), core, 0)
    whole = jnp.concatenate([keep, lax.ppermute(give, "ao", near)], 2)
    both = product("tbn,nd->tbd", whole, side_rows).astype(BF16)
    dressed = both[:, :, :2 * vir_part] + lax.ppermute(both[:, :, 2 * vir_part:], "ao", far)
    both = product("otid,tbd->otib", arrived, dressed).astype(BF16)
    here, there = split(both, part // 2, 3)
    summed = here + lax.ppermute(there, "ao", far)
    back = lax.all_to_all(summed, "occ", split_axis=0, concat_axis=0, tiled=True)
    total = product("ota,otib->iab", target_rows, back).astype(BF16)
    keep, give = split(total, core, 2)
    return keep + lax.ppermute(give, "ao", near)


def solution(mesh):
    placed = (P("occ", None, "ao"), P(), P("occ", None, "ao"), P(), P(), P(), P())

    def whole(amplitudes, *rest):
        nodes = mesh.shape["occ"]
        rows = amplitudes.shape[0] // nodes
        body = shards if rows % 16 == 0 and nodes <= 16 else plain_shards
        return jax.shard_map(
            body, mesh=mesh, in_specs=placed, out_specs=P("occ", None, "ao"), check_vma=False
        )(amplitudes, *rest)

    return whole
```

```python
import functools

import jax
import jax.numpy as jnp
from jax import lax
from jax.experimental import pallas as pl
from jax.experimental.pallas import tpu as pltpu
from jax.sharding import PartitionSpec as P

F32, BF16 = jnp.float32, jnp.bfloat16
TILE_PARTS = 4
VMEM_LIMIT = 16 * 1024 * 1024
TILE_VMEM_LIMIT = 50 * 1024 * 1024


def dot(a, b, dims=(((1,), (0,)), ((), ()))):
    return lax.dot_general(a, b, dims, preferred_element_type=F32)


def call(body, outs, ins, flops, scratch=(), early=(), limit=VMEM_LIMIT):
    whole = pl.BlockSpec(memory_space=pltpu.VMEM)
    moved = sum(2 * x.size for x in ins) + sum(2 * x.size for x in outs)
    return pl.pallas_call(
        body,
        out_shape=outs,
        in_specs=[whole] * len(ins) + [pl.BlockSpec(memory_space=pl.ANY)] * len(early),
        out_specs=[whole] * len(outs),
        scratch_shapes=list(scratch),
        cost_estimate=pl.CostEstimate(flops=flops, bytes_accessed=moved, transcendentals=0),
        compiler_params=pltpu.CompilerParams(vmem_limit_bytes=limit),
    )(*ins, *early)


def order_orbitals(orbitals, left, side_rows, held):
    vir = orbitals.shape[1]
    part = lax.axis_index("ao")
    nu_part = side_rows.shape[0] // 2
    line = orbitals[...]
    left[...] = line.T
    quarters = [line[:, q:q + vir // 4] for q in (vir // 4, 0, 3 * vir // 4, vir // 2)]
    line = jnp.where(part % 2 == 0, line, jnp.concatenate(quarters, 1))
    line = jnp.where(part // 2 == 0, line, jnp.concatenate([line[:, vir // 2:], line[:, :vir // 2]], 1))
    held[...] = line
    for q in range(2):
        start = pl.multiple_of((part ^ q) * nu_part, nu_part)
        side_rows[pl.ds(q * nu_part, nu_part), :] = held[pl.ds(start, nu_part), :]


def source_body(src, sub, orbitals, early, source, held, ahead):
    held[...] = orbitals[...].astype(F32)
    nodes = lax.axis_size("occ")
    slots = src.shape[0] // nodes
    half = slots // 2
    blocks = held.shape[0] // nodes
    core = lax.axis_index("ao") % 2
    for k in range(nodes):

        def step(j, carry):
            slot = k * slots + core * half + j
            ahead[pl.ds(k * half + j, 1), :] = held[pl.ds(src[slot] * blocks + sub[slot], 1), :]
            return carry

        lax.fori_loop(0, half, step, 0, unroll=8)
    source[...] = ahead[...].astype(BF16)


def target_body(row, count, orbitals, early, target, held, back):
    held[...] = orbitals[...].astype(F32)
    nodes = count.shape[0]
    slots = row.shape[0] // nodes
    half = slots // 2
    blocks = held.shape[0] // nodes
    own, core = lax.axis_index("occ"), lax.axis_index("ao") % 2
    for k in range(nodes):
        partner = own ^ k

        def step(j, carry):
            place = core * half + j
            line = held[pl.ds(partner * blocks + row[partner * slots + place], 1), :]
            back[pl.ds(k * half + j, 1), :] = jnp.where(place < count[partner], line, 0.0)
            return carry

        lax.fori_loop(0, half, step, 0, unroll=8)
    target[...] = back[...].astype(BF16)


def gather(body, tables, orbitals, early):
    slots, vir = tables[0].shape[0] // 2, orbitals.shape[1]
    scalar = pl.BlockSpec(memory_space=pltpu.SMEM)
    whole = pl.BlockSpec(memory_space=pltpu.VMEM)
    return pl.pallas_call(
        body,
        out_shape=jax.ShapeDtypeStruct((slots, vir), BF16),
        in_specs=[scalar] * 2 + [whole, pl.BlockSpec(memory_space=pl.ANY)],
        out_specs=whole,
        scratch_shapes=[pltpu.VMEM(orbitals.shape, F32), pltpu.VMEM((slots, vir), F32)],
        cost_estimate=pl.CostEstimate(flops=slots * vir, bytes_accessed=4 * slots * vir, transcendentals=0),
        compiler_params=pltpu.CompilerParams(vmem_limit_bytes=VMEM_LIMIT),
    )(*tables, orbitals, early)


def rows_body(rows_ref, mine_ref, other_ref, *rest):
    out, held, sems = rest[-3:]
    nodes, occ, slots, width = held.shape
    rows = rows_ref[...]
    copies = []
    part = occ // sems.shape[0]
    for s in range(sems.shape[0]):
        for i in range(s * part, (s + 1) * part, 2):
            right = jnp.concatenate([mine_ref[i], other_ref[i], mine_ref[i + 1], other_ref[i + 1]], 0)
            product = dot(rows, right, (((1,), (1,)), ((), ()))).astype(BF16)
            for j in range(2):
                held[:, i + j] = product[:, j * width:(j + 1) * width].reshape(nodes, slots, width)
        piece = pl.ds(s * part, part)
        copies.append(pltpu.make_async_copy(held.at[:, piece], out.at[:, piece], sems.at[s]))
        copies[-1].start()
    for copy in copies:
        copy.wait()


def pair_rows(rows, mine, other, nodes, early):
    occ, part, vir = mine.shape
    count = rows.shape[0]
    shape = (nodes, occ, count // nodes, 2 * part)
    whole = pl.BlockSpec(memory_space=pltpu.VMEM)
    away = pl.BlockSpec(memory_space=pl.ANY)
    return pl.pallas_call(
        rows_body,
        out_shape=jax.ShapeDtypeStruct(shape, BF16),
        in_specs=[whole] * 3 + [away] * len(early),
        out_specs=pl.BlockSpec(memory_space=pltpu.HBM),
        scratch_shapes=[pltpu.VMEM(shape, BF16), pltpu.SemaphoreType.DMA((4,))],
        cost_estimate=pl.CostEstimate(
            flops=4 * count * occ * vir * part, bytes_accessed=4 * occ * part * vir, transcendentals=0
        ),
        compiler_params=pltpu.CompilerParams(vmem_limit_bytes=TILE_VMEM_LIMIT),
    )(rows, mine, other, *early)


def turn_body(groups, meta, *refs):
    blocks, (out, held) = refs[:groups], refs[-2:]
    _, occ, slots, width = blocks[0].shape
    for n in range(groups):
        base = n * occ * slots
        held[base:base + occ * slots, :] = blocks[n][0].astype(F32).reshape(occ * slots, width)
        for t in range(slots):
            out[n, t] = held[pl.ds(base + t, occ, stride=slots), :].astype(BF16)


def turn(own, arrived, partners, early):
    groups = len(partners)
    _, occ, slots, width = arrived.shape
    specs = [
        pl.BlockSpec((1, occ, slots, width), lambda n, ref, k=k: (ref[0] ^ k, 0, 0, 0)) for k in partners
    ]
    return pl.pallas_call(
        functools.partial(turn_body, groups),
        out_shape=jax.ShapeDtypeStruct((groups, slots, occ, width), BF16),
        grid_spec=pltpu.PrefetchScalarGridSpec(
            num_scalar_prefetch=1,
            grid=(1,),
            in_specs=specs + [pl.BlockSpec(memory_space=pl.ANY)] * len(early),
            out_specs=pl.BlockSpec(memory_space=pltpu.VMEM),
            scratch_shapes=[pltpu.VMEM((groups * occ * slots, width), F32)],
        ),
        cost_estimate=pl.CostEstimate(
            flops=groups * occ * slots * width, bytes_accessed=4 * groups * occ * slots * width, transcendentals=0
        ),
        compiler_params=pltpu.CompilerParams(vmem_limit_bytes=VMEM_LIMIT),
    )(jnp.reshape(own, (1,)), *[arrived] * groups, *early)


def start_copies(other_core, start, tiles, held, sems):
    core = lax.axis_index("ao") % 2
    offset = (1 - core if other_core else core) * (tiles.shape[0] // 2) + start
    pieces = sems.shape[0]
    size = held.shape[0] // pieces
    copies = []
    for n in range(pieces):
        source = tiles.at[pl.ds(offset + n * size, size)]
        copies.append(pltpu.make_async_copy(source, held.at[pl.ds(n * size, size)], sems.at[n]))
        copies[n].start()
    return copies


def pair_dot(left, held, t):
    product = dot(left, jnp.concatenate([held[t], held[t + 1]], 1))
    width = held.shape[2]
    return product[:, :width].astype(BF16), product[:, width:].astype(BF16)


def transform_tiles(left_ref, copies, held, out):
    size = out.shape[0] // len(copies)
    left = left_ref[...]
    for n, copy in enumerate(copies):
        copy.wait()
        for t in range(n * size, (n + 1) * size, 2):
            out[t], out[t + 1] = pair_dot(left, held, t)


def give_kernel(start, left_ref, tiles, *rest):
    out, held, sems = rest[-3:]
    transform_tiles(left_ref, start_copies(True, start, tiles, held, sems), held, out)


def first_kernel(start, orbitals, tiles, out, left_ref, side_rows, held, sems, lines):
    copies = start_copies(True, start, tiles, held, sems)
    order_orbitals(orbitals, left_ref, side_rows, lines)
    transform_tiles(left_ref, copies, held, out)


def finish_kernel(start, skip, left_ref, tiles, other, right_ref, *rest):
    here, there, held, sems = rest[-4:]
    copies = start_copies(False, start, tiles, held, sems)
    size = here.shape[0] // len(copies)
    width = here.shape[1]
    left, right = left_ref[...], right_ref[...]
    side = lax.axis_index("ao") // 2
    for n, copy in enumerate(copies):
        copy.wait()
        rows = []
        for t in range(n * size, (n + 1) * size, 2):
            for j, mine in enumerate(pair_dot(left, held, t)):
                rows.append(jnp.concatenate([mine, other[skip + t + j]], 1))
        both = dot(jnp.concatenate(rows, 0), right).reshape(size, -1, right.shape[1]).astype(BF16)
        piece = pl.ds(n * size, size)
        low, high = both[:, :width], both[:, width:]
        here[piece] = jnp.where(side == 0, low, high)
        away = jnp.where(side == 0, high, low)
        there[piece] = jnp.concatenate([away[:, :, width:], away[:, :, :width]], 2)


PIECE = 4


def tile_call(body, count, tiles, ins, outs, early=(), scratch=()):
    _, sig, nu = tiles.shape
    vir = outs[0].shape[1]
    whole = pl.BlockSpec(memory_space=pltpu.VMEM)
    away = pl.BlockSpec(memory_space=pl.ANY)
    flops = 2 * count * vir * nu * (sig + 2 * vir * (len(outs) - 1))
    return pl.pallas_call(
        body,
        out_shape=outs,
        in_specs=[whole, away] + [whole] * (len(ins) - 1) + [away] * len(early),
        out_specs=[whole] * len(outs),
        scratch_shapes=[pltpu.VMEM((count, sig, nu), BF16), pltpu.SemaphoreType.DMA((count // PIECE,)), *scratch],
        cost_estimate=pl.CostEstimate(
            flops=flops, bytes_accessed=2 * count * sig * nu * 2, transcendentals=0
        ),
        compiler_params=pltpu.CompilerParams(vmem_limit_bytes=TILE_VMEM_LIMIT),
    )(ins[0], tiles, *ins[1:], *early)


def dress_body(parts, *refs):
    out = refs[-1]
    t = 0
    for n in range(parts):
        size = refs[2 * n].shape[0]
        out[t:t + size] = refs[2 * n][...] + refs[2 * n + 1][...]
        t += size


def dress(parts):
    slots = sum(x.shape[0] for x in parts[::2])
    outs = [jax.ShapeDtypeStruct((slots,) + parts[0].shape[1:], BF16)]
    return call(functools.partial(dress_body, len(parts) // 2), outs, parts, slots)[0]


def product_body(near_ref, far_ref, dressed, last, last_far, *refs):
    scratch = refs[-1]
    groups, slots, occ, _ = near_ref.shape
    outs = refs[-1 - groups:-1]
    first = dressed.shape[0]
    for t in range(slots):
        tile = dressed[t] if t < first else last[t - first] + last_far[t - first]
        rows = [jnp.concatenate([near_ref[n, t], far_ref[n, t]], 1) for n in range(groups)]
        product = dot(jnp.concatenate(rows, 0), tile, (((1,), (1,)), ((), ())))
        scratch[pl.ds(t, groups * occ, stride=slots), :] = product
    for n, out in enumerate(outs):
        block = occ * slots
        out[...] = scratch[n * block:(n + 1) * block, :].reshape(out.shape).astype(BF16)


def products(near_rows, far_rows, tiles, early):
    groups, slots, occ, width = near_rows.shape
    outs = [jax.ShapeDtypeStruct((occ, slots, width), BF16)] * groups
    scratch = [pltpu.VMEM((groups * occ * slots, width), F32)]
    flops = 4 * groups * occ * slots * width * width
    return call(product_body, outs, (near_rows, far_rows, *tiles), flops, scratch, early)


def copy_body(rows, *rest):
    rest[-1][...] = rows[...]


def rows_after(rows, early):
    return call(copy_body, [jax.ShapeDtypeStruct(rows.shape, BF16)], (rows,), rows.size, (), early)[0]


def back_body(nodes, rows_ref, *refs):
    values, (keep, give) = refs[:nodes], refs[nodes:]
    occ = values[0].shape[0]
    part = keep.shape[1]
    core = lax.axis_index("ao") % 2
    rows = rows_ref[...]

    def step(i, carry):
        left = jnp.concatenate([v[i] for v in values], 0)
        product = dot(left, rows, (((0,), (0,)), ((), ())))
        low, high = product[:part].astype(BF16), product[part:].astype(BF16)
        keep[i] = jnp.where(core == 0, low, high)
        give[i] = jnp.where(core == 0, high, low)
        return carry

    lax.fori_loop(0, occ, step, 0, unroll=4)


def back_transform(rows, values):
    occ, _, width = values[0].shape
    count, vir = rows.shape
    outs = [jax.ShapeDtypeStruct((occ, width // 2, vir), BF16)] * 2
    return call(
        functools.partial(back_body, len(values)), outs, (rows, *values), 2 * occ * vir * count * width
    )


def shards(amplitudes, orbitals, tiles, tile_count, tile_row, tile_src, tile_sub):
    nodes = lax.axis_size("occ")
    own = lax.axis_index("occ")
    parts = lax.axis_size("ao")
    part = lax.axis_index("ao")
    core = part % 2
    near = [(q, q ^ 1) for q in range(parts)]
    far = [(q, q ^ 2) for q in range(parts)]
    local_occ, vir, vir_part = amplitudes.shape
    nu_part = tiles.shape[2]
    slots = tiles.shape[0]
    half = slots // 2
    blocks = orbitals.shape[0] // nodes
    pick = lax.dynamic_slice_in_dim

    mine = jnp.swapaxes(amplitudes, 1, 2)
    other = lax.ppermute(mine, "ao", near)
    def tile_shape(count, width):
        return jax.ShapeDtypeStruct((count, vir, width), BF16)

    def give(start, early):
        outs = [tile_shape(half // 2, nu_part)]
        body = functools.partial(give_kernel, start)
        (given,) = tile_call(body, half // 2, tiles, (left,), outs, early)
        return given, lax.ppermute(given, "ao", near)

    outs = [
        tile_shape(half // 2, nu_part),
        jax.ShapeDtypeStruct((vir, orbitals.shape[0]), BF16),
        jax.ShapeDtypeStruct((2 * nu_part, vir), BF16),
    ]
    scratch = [pltpu.VMEM(orbitals.shape, BF16)]
    given, left, side_rows = tile_call(
        functools.partial(first_kernel, 0), half // 2, tiles, (orbitals,), outs, (), scratch
    )
    first_parts = lax.ppermute(given, "ao", near)
    given, second_parts = give(half // 2, [given, other])
    source_rows = gather(source_body, (tile_src[:, 0], tile_sub), orbitals, given)
    sent = pair_rows(source_rows, mine, other, nodes, (first_parts, second_parts))
    arrived = lax.all_to_all(sent, "occ", split_axis=0, concat_axis=0, tiled=True)
    parts, early = [], [sent]
    step = half // TILE_PARTS
    for n in range(TILE_PARTS):
        if n >= 2:
            early.append(parts[2 * n - 3])
        other_parts = first_parts if 2 * n < TILE_PARTS else second_parts
        here, there = tile_call(
            functools.partial(finish_kernel, n * step, n * step % (half // 2)), step, tiles,
            (left, other_parts, side_rows), [jax.ShapeDtypeStruct((step, vir // 2, vir), BF16)] * 2, early,
        )
        early = [there]
        parts += [here, lax.ppermute(there, "ao", far)]
    target_rows = gather(target_body, (tile_row, tile_count), orbitals, early[0])
    tiles_done = [dress(parts[:-2]), *parts[-2:]]
    lower = nodes // 2
    light = [k for k in ((n + lower // 2) % lower for n in range(lower)) if k] + [0]
    units = [[nodes - 1]]
    for n in range(1, lower):
        units += [[nodes - 1 - n], [light[n - 1]]]
    units.append([light[-1]])
    wait_for = {4: (0,), 5: (1,), 6: (2, 3)}
    blocks_of, far_blocks = [], []
    for unit in units:
        blocks_of.append(turn(own, arrived, unit, blocks_of[-1:]))
        far_blocks.append(lax.ppermute(blocks_of[-1], "ao", far))
    returned, made = {}, []
    for n, unit in enumerate(units):
        early = list(made[:1]) + [returned[k] for m in wait_for.get(n, ()) for k in units[m]]
        made = products(blocks_of[n], far_blocks[n], tiles_done, early)
        for k, x in zip(unit, made):
            returned[k] = lax.ppermute(x, "occ", [(o, o ^ k) for o in range(nodes)]) if k else x
    late = [returned[k] for m in (5, 4) if m < len(units) for k in units[m]]
    target_rows = rows_after(target_rows, late)
    returned = [returned[k] for k in range(nodes)]
    keep, give_up = back_transform(target_rows, returned)
    return jnp.swapaxes(keep + lax.ppermute(give_up, "ao", near), 1, 2)


def plain_shards(amplitudes, orbitals, tiles, tile_count, tile_row, tile_src, tile_sub):
    nodes = lax.axis_size("occ")
    parts = lax.axis_size("ao")
    part = lax.axis_index("ao")
    core = part % 2
    near = [(q, q ^ 1) for q in range(parts)]
    far = [(q, q ^ 2) for q in range(parts)]
    vir_part = amplitudes.shape[2]
    nu_part = tiles.shape[2]
    slots = tiles.shape[0]
    half = slots // 2
    blocks = orbitals.shape[0] // nodes
    pick = lax.dynamic_slice_in_dim
    ordered = jnp.concatenate([pick(orbitals, (part ^ q) * vir_part, vir_part, 1) for q in range(parts)], 1)
    side_rows = jnp.concatenate([pick(ordered, (part ^ q) * nu_part, nu_part, 0) for q in range(2)], 0)

    def mine_of(table):
        return pick(table.reshape(nodes, slots), core * half, half, 1)

    def product(form, a, b):
        return jnp.einsum(form, a, b, preferred_element_type=F32)

    def split(x, at, axis):
        size = x.shape[axis] // 2
        return pick(x, at * size, size, axis), pick(x, (1 - at) * size, size, axis)

    source = mine_of(tile_src[:, 0]) * blocks + mine_of(tile_sub)
    target = jnp.arange(nodes, dtype=jnp.int32)[:, None] * blocks + mine_of(tile_row)
    place = core * half + jnp.arange(half, dtype=jnp.int32)
    live = place[None, :] < tile_count[:, None]
    source_rows = jnp.take(orbitals, source, axis=0)
    target_rows = jnp.where(live[:, :, None], jnp.take(orbitals, target, axis=0), 0)
    paired = jnp.concatenate([amplitudes, lax.ppermute(amplitudes, "ao", near)], 2)
    sent = product("otc,icd->otid", source_rows, paired).astype(BF16)
    arrived = lax.all_to_all(sent, "occ", split_axis=0, concat_axis=0, tiled=True)
    keep, give = split(product("sb,tsn->tbn", orbitals, tiles).astype(BF16), core, 0)
    whole = jnp.concatenate([keep, lax.ppermute(give, "ao", near)], 2)
    both = product("tbn,nd->tbd", whole, side_rows).astype(BF16)
    dressed = both[:, :, :2 * vir_part] + lax.ppermute(both[:, :, 2 * vir_part:], "ao", far)
    both = product("otid,tbd->otib", arrived, dressed).astype(BF16)
    here, there = split(both, part // 2, 3)
    summed = here + lax.ppermute(there, "ao", far)
    back = lax.all_to_all(summed, "occ", split_axis=0, concat_axis=0, tiled=True)
    total = product("ota,otib->iab", target_rows, back).astype(BF16)
    keep, give = split(total, core, 2)
    return keep + lax.ppermute(give, "ao", near)


def solution(mesh):
    placed = (P("occ", None, "ao"), P(), P("occ", None, "ao"), P(), P(), P(), P())

    def whole(amplitudes, *rest):
        nodes = mesh.shape["occ"]
        rows = amplitudes.shape[0] // nodes
        few = nodes <= 16 and nodes & (nodes - 1) == 0
        body = shards if few and rows % 16 == 0 else plain_shards
        return jax.shard_map(
            body, mesh=mesh, in_specs=placed, out_specs=P("occ", None, "ao"), check_vma=False
        )(amplitudes, *rest)

    return whole
```

```python
import functools

import jax
import jax.numpy as jnp
from jax import lax
from jax.experimental import pallas as pl
from jax.experimental.pallas import tpu as pltpu
from jax.sharding import PartitionSpec as P

F32, BF16 = jnp.float32, jnp.bfloat16
TILE_PARTS = 4
VMEM_LIMIT = 16 * 1024 * 1024
TILE_VMEM_LIMIT = 50 * 1024 * 1024


def dot(a, b, dims=(((1,), (0,)), ((), ()))):
    return lax.dot_general(a, b, dims, preferred_element_type=F32)


def call(body, outs, ins, flops, scratch=(), early=(), limit=VMEM_LIMIT):
    whole = pl.BlockSpec(memory_space=pltpu.VMEM)
    moved = sum(2 * x.size for x in ins) + sum(2 * x.size for x in outs)
    return pl.pallas_call(
        body,
        out_shape=outs,
        in_specs=[whole] * len(ins) + [pl.BlockSpec(memory_space=pl.ANY)] * len(early),
        out_specs=[whole] * len(outs),
        scratch_shapes=list(scratch),
        cost_estimate=pl.CostEstimate(flops=flops, bytes_accessed=moved, transcendentals=0),
        compiler_params=pltpu.CompilerParams(vmem_limit_bytes=limit),
    )(*ins, *early)


def order_orbitals(orbitals, left, side_rows, held):
    vir = orbitals.shape[1]
    part = lax.axis_index("ao")
    nu_part = side_rows.shape[0] // 2
    line = orbitals[...]
    left[...] = line.T
    quarters = [line[:, q:q + vir // 4] for q in (vir // 4, 0, 3 * vir // 4, vir // 2)]
    line = jnp.where(part % 2 == 0, line, jnp.concatenate(quarters, 1))
    line = jnp.where(part // 2 == 0, line, jnp.concatenate([line[:, vir // 2:], line[:, :vir // 2]], 1))
    held[...] = line
    for q in range(2):
        start = pl.multiple_of((part ^ q) * nu_part, nu_part)
        side_rows[pl.ds(q * nu_part, nu_part), :] = held[pl.ds(start, nu_part), :]


def source_body(src, sub, orbitals, early, source, held, ahead):
    held[...] = orbitals[...].astype(F32)
    nodes = lax.axis_size("occ")
    slots = src.shape[0] // nodes
    half = slots // 2
    blocks = held.shape[0] // nodes
    core = lax.axis_index("ao") % 2
    for k in range(nodes):

        def step(j, carry):
            slot = k * slots + core * half + j
            ahead[pl.ds(k * half + j, 1), :] = held[pl.ds(src[slot] * blocks + sub[slot], 1), :]
            return carry

        lax.fori_loop(0, half, step, 0, unroll=8)
    source[...] = ahead[...].astype(BF16)


def target_body(row, count, orbitals, early, target, held, back):
    held[...] = orbitals[...].astype(F32)
    nodes = count.shape[0]
    slots = row.shape[0] // nodes
    half = slots // 2
    blocks = held.shape[0] // nodes
    own, core = lax.axis_index("occ"), lax.axis_index("ao") % 2
    for k in range(nodes):
        partner = own ^ k

        def step(j, carry):
            place = core * half + j
            line = held[pl.ds(partner * blocks + row[partner * slots + place], 1), :]
            back[pl.ds(k * half + j, 1), :] = jnp.where(place < count[partner], line, 0.0)
            return carry

        lax.fori_loop(0, half, step, 0, unroll=8)
    target[...] = back[...].astype(BF16)


def gather(body, tables, orbitals, early):
    slots, vir = tables[0].shape[0] // 2, orbitals.shape[1]
    scalar = pl.BlockSpec(memory_space=pltpu.SMEM)
    whole = pl.BlockSpec(memory_space=pltpu.VMEM)
    return pl.pallas_call(
        body,
        out_shape=jax.ShapeDtypeStruct((slots, vir), BF16),
        in_specs=[scalar] * 2 + [whole, pl.BlockSpec(memory_space=pl.ANY)],
        out_specs=whole,
        scratch_shapes=[pltpu.VMEM(orbitals.shape, F32), pltpu.VMEM((slots, vir), F32)],
        cost_estimate=pl.CostEstimate(flops=slots * vir, bytes_accessed=4 * slots * vir, transcendentals=0),
        compiler_params=pltpu.CompilerParams(vmem_limit_bytes=VMEM_LIMIT),
    )(*tables, orbitals, early)


def rows_body(rows_ref, mine_ref, other_ref, *rest):
    out, held, sems = rest[-3:]
    nodes, occ, slots, width = held.shape
    rows = rows_ref[...]
    copies = []
    part = occ // sems.shape[0]
    for s in range(sems.shape[0]):
        for i in range(s * part, (s + 1) * part, 2):
            right = jnp.concatenate([mine_ref[i], other_ref[i], mine_ref[i + 1], other_ref[i + 1]], 0)
            product = dot(rows, right, (((1,), (1,)), ((), ()))).astype(BF16)
            for j in range(2):
                held[:, i + j] = product[:, j * width:(j + 1) * width].reshape(nodes, slots, width)
        piece = pl.ds(s * part, part)
        copies.append(pltpu.make_async_copy(held.at[:, piece], out.at[:, piece], sems.at[s]))
        copies[-1].start()
    for copy in copies:
        copy.wait()


def pair_rows(rows, mine, other, nodes, early):
    occ, part, vir = mine.shape
    count = rows.shape[0]
    shape = (nodes, occ, count // nodes, 2 * part)
    whole = pl.BlockSpec(memory_space=pltpu.VMEM)
    away = pl.BlockSpec(memory_space=pl.ANY)
    return pl.pallas_call(
        rows_body,
        out_shape=jax.ShapeDtypeStruct(shape, BF16),
        in_specs=[whole] * 3 + [away] * len(early),
        out_specs=pl.BlockSpec(memory_space=pltpu.HBM),
        scratch_shapes=[pltpu.VMEM(shape, BF16), pltpu.SemaphoreType.DMA((4,))],
        cost_estimate=pl.CostEstimate(
            flops=4 * count * occ * vir * part, bytes_accessed=4 * occ * part * vir, transcendentals=0
        ),
        compiler_params=pltpu.CompilerParams(vmem_limit_bytes=TILE_VMEM_LIMIT),
    )(rows, mine, other, *early)


def turn_body(groups, meta, *refs):
    blocks, (out, held) = refs[:groups], refs[-2:]
    _, occ, slots, width = blocks[0].shape
    for n in range(groups):
        base = n * occ * slots
        held[base:base + occ * slots, :] = blocks[n][0].astype(F32).reshape(occ * slots, width)
        for t in range(slots):
            out[n, t] = held[pl.ds(base + t, occ, stride=slots), :].astype(BF16)


def turn(own, arrived, partners, early):
    groups = len(partners)
    _, occ, slots, width = arrived.shape
    specs = [
        pl.BlockSpec((1, occ, slots, width), lambda n, ref, k=k: (ref[0] ^ k, 0, 0, 0)) for k in partners
    ]
    return pl.pallas_call(
        functools.partial(turn_body, groups),
        out_shape=jax.ShapeDtypeStruct((groups, slots, occ, width), BF16),
        grid_spec=pltpu.PrefetchScalarGridSpec(
            num_scalar_prefetch=1,
            grid=(1,),
            in_specs=specs + [pl.BlockSpec(memory_space=pl.ANY)] * len(early),
            out_specs=pl.BlockSpec(memory_space=pltpu.VMEM),
            scratch_shapes=[pltpu.VMEM((groups * occ * slots, width), F32)],
        ),
        cost_estimate=pl.CostEstimate(
            flops=groups * occ * slots * width, bytes_accessed=4 * groups * occ * slots * width, transcendentals=0
        ),
        compiler_params=pltpu.CompilerParams(vmem_limit_bytes=VMEM_LIMIT),
    )(jnp.reshape(own, (1,)), *[arrived] * groups, *early)


def start_copies(other_core, start, tiles, held, sems):
    core = lax.axis_index("ao") % 2
    offset = (1 - core if other_core else core) * (tiles.shape[0] // 2) + start
    pieces = sems.shape[0]
    size = held.shape[0] // pieces
    copies = []
    for n in range(pieces):
        source = tiles.at[pl.ds(offset + n * size, size)]
        copies.append(pltpu.make_async_copy(source, held.at[pl.ds(n * size, size)], sems.at[n]))
        copies[n].start()
    return copies


def pair_dot(left, held, t):
    product = dot(left, jnp.concatenate([held[t], held[t + 1]], 1))
    width = held.shape[2]
    return product[:, :width].astype(BF16), product[:, width:].astype(BF16)


def transform_tiles(left_ref, copies, held, out):
    size = out.shape[0] // len(copies)
    left = left_ref[...]
    for n, copy in enumerate(copies):
        copy.wait()
        for t in range(n * size, (n + 1) * size, 2):
            out[t], out[t + 1] = pair_dot(left, held, t)


def give_kernel(start, left_ref, tiles, *rest):
    out, held, sems = rest[-3:]
    transform_tiles(left_ref, start_copies(True, start, tiles, held, sems), held, out)


def first_kernel(start, orbitals, tiles, out, left_ref, side_rows, held, sems, lines):
    copies = start_copies(True, start, tiles, held, sems)
    order_orbitals(orbitals, left_ref, side_rows, lines)
    transform_tiles(left_ref, copies, held, out)


def finish_kernel(start, skip, left_ref, tiles, other, right_ref, *rest):
    here, there, held, sems = rest[-4:]
    copies = start_copies(False, start, tiles, held, sems)
    size = here.shape[0] // len(copies)
    width = here.shape[1]
    left, right = left_ref[...], right_ref[...]
    side = lax.axis_index("ao") // 2
    for n, copy in enumerate(copies):
        copy.wait()
        rows = []
        for t in range(n * size, (n + 1) * size, 2):
            for j, mine in enumerate(pair_dot(left, held, t)):
                rows.append(jnp.concatenate([mine, other[skip + t + j]], 1))
        both = dot(jnp.concatenate(rows, 0), right).reshape(size, -1, right.shape[1]).astype(BF16)
        piece = pl.ds(n * size, size)
        low, high = both[:, :width], both[:, width:]
        here[piece] = jnp.where(side == 0, low, high)
        away = jnp.where(side == 0, high, low)
        there[piece] = jnp.concatenate([away[:, :, width:], away[:, :, :width]], 2)


PIECE = 8


def tile_call(body, count, tiles, ins, outs, early=(), scratch=()):
    _, sig, nu = tiles.shape
    vir = outs[0].shape[1]
    whole = pl.BlockSpec(memory_space=pltpu.VMEM)
    away = pl.BlockSpec(memory_space=pl.ANY)
    flops = 2 * count * vir * nu * (sig + 2 * vir * (len(outs) - 1))
    return pl.pallas_call(
        body,
        out_shape=outs,
        in_specs=[whole, away] + [whole] * (len(ins) - 1) + [away] * len(early),
        out_specs=[whole] * len(outs),
        scratch_shapes=[pltpu.VMEM((count, sig, nu), BF16), pltpu.SemaphoreType.DMA((count // PIECE,)), *scratch],
        cost_estimate=pl.CostEstimate(
            flops=flops, bytes_accessed=2 * count * sig * nu * 2, transcendentals=0
        ),
        compiler_params=pltpu.CompilerParams(vmem_limit_bytes=TILE_VMEM_LIMIT),
    )(ins[0], tiles, *ins[1:], *early)


def dress_body(parts, *refs):
    out = refs[-1]
    t = 0
    for n in range(parts):
        size = refs[2 * n].shape[0]
        out[t:t + size] = refs[2 * n][...] + refs[2 * n + 1][...]
        t += size


def dress(parts):
    slots = sum(x.shape[0] for x in parts[::2])
    outs = [jax.ShapeDtypeStruct((slots,) + parts[0].shape[1:], BF16)]
    return call(functools.partial(dress_body, len(parts) // 2), outs, parts, slots)[0]


def product_body(near_ref, far_ref, dressed, last, last_far, *refs):
    scratch = refs[-1]
    groups, slots, occ, _ = near_ref.shape
    outs = refs[-1 - groups:-1]
    first = dressed.shape[0]
    for t in range(slots):
        tile = dressed[t] if t < first else last[t - first] + last_far[t - first]
        rows = [jnp.concatenate([near_ref[n, t], far_ref[n, t]], 1) for n in range(groups)]
        product = dot(jnp.concatenate(rows, 0), tile, (((1,), (1,)), ((), ())))
        scratch[pl.ds(t, groups * occ, stride=slots), :] = product
    for n, out in enumerate(outs):
        block = occ * slots
        out[...] = scratch[n * block:(n + 1) * block, :].reshape(out.shape).astype(BF16)


def products(near_rows, far_rows, tiles, early):
    groups, slots, occ, width = near_rows.shape
    outs = [jax.ShapeDtypeStruct((occ, slots, width), BF16)] * groups
    scratch = [pltpu.VMEM((groups * occ * slots, width), F32)]
    flops = 4 * groups * occ * slots * width * width
    return call(product_body, outs, (near_rows, far_rows, *tiles), flops, scratch, early)


def copy_body(rows, *rest):
    rest[-1][...] = rows[...]


def rows_after(rows, early):
    return call(copy_body, [jax.ShapeDtypeStruct(rows.shape, BF16)], (rows,), rows.size, (), early)[0]


def back_body(nodes, rows_ref, *refs):
    values, (keep, give) = refs[:nodes], refs[nodes:]
    occ = values[0].shape[0]
    part = keep.shape[1]
    core = lax.axis_index("ao") % 2
    rows = rows_ref[...]

    def step(i, carry):
        left = jnp.concatenate([v[i] for v in values], 0)
        product = dot(left, rows, (((0,), (0,)), ((), ())))
        low, high = product[:part].astype(BF16), product[part:].astype(BF16)
        keep[i] = jnp.where(core == 0, low, high)
        give[i] = jnp.where(core == 0, high, low)
        return carry

    lax.fori_loop(0, occ, step, 0, unroll=8)


def back_transform(rows, values):
    occ, _, width = values[0].shape
    count, vir = rows.shape
    outs = [jax.ShapeDtypeStruct((occ, width // 2, vir), BF16)] * 2
    return call(
        functools.partial(back_body, len(values)), outs, (rows, *values), 2 * occ * vir * count * width
    )


def shards(amplitudes, orbitals, tiles, tile_count, tile_row, tile_src, tile_sub):
    nodes = lax.axis_size("occ")
    own = lax.axis_index("occ")
    parts = lax.axis_size("ao")
    part = lax.axis_index("ao")
    core = part % 2
    near = [(q, q ^ 1) for q in range(parts)]
    far = [(q, q ^ 2) for q in range(parts)]
    local_occ, vir, vir_part = amplitudes.shape
    nu_part = tiles.shape[2]
    slots = tiles.shape[0]
    half = slots // 2
    blocks = orbitals.shape[0] // nodes
    pick = lax.dynamic_slice_in_dim

    mine = jnp.swapaxes(amplitudes, 1, 2)
    other = lax.ppermute(mine, "ao", near)
    def tile_shape(count, width):
        return jax.ShapeDtypeStruct((count, vir, width), BF16)

    def give(start, early):
        outs = [tile_shape(half // 2, nu_part)]
        body = functools.partial(give_kernel, start)
        (given,) = tile_call(body, half // 2, tiles, (left,), outs, early)
        return given, lax.ppermute(given, "ao", near)

    outs = [
        tile_shape(half // 2, nu_part),
        jax.ShapeDtypeStruct((vir, orbitals.shape[0]), BF16),
        jax.ShapeDtypeStruct((2 * nu_part, vir), BF16),
    ]
    scratch = [pltpu.VMEM(orbitals.shape, BF16)]
    given, left, side_rows = tile_call(
        functools.partial(first_kernel, 0), half // 2, tiles, (orbitals,), outs, (), scratch
    )
    first_parts = lax.ppermute(given, "ao", near)
    given, second_parts = give(half // 2, [given, other])
    source_rows = gather(source_body, (tile_src[:, 0], tile_sub), orbitals, given)
    sent = pair_rows(source_rows, mine, other, nodes, (first_parts, second_parts))
    arrived = lax.all_to_all(sent, "occ", split_axis=0, concat_axis=0, tiled=True)
    parts, early = [], [sent]
    step = half // TILE_PARTS
    for n in range(TILE_PARTS):
        if n >= 2:
            early.append(parts[2 * n - 3])
        other_parts = first_parts if 2 * n < TILE_PARTS else second_parts
        here, there = tile_call(
            functools.partial(finish_kernel, n * step, n * step % (half // 2)), step, tiles,
            (left, other_parts, side_rows), [jax.ShapeDtypeStruct((step, vir // 2, vir), BF16)] * 2, early,
        )
        early = [there]
        parts += [here, lax.ppermute(there, "ao", far)]
    target_rows = gather(target_body, (tile_row, tile_count), orbitals, early[0])
    tiles_done = [dress(parts[:-2]), *parts[-2:]]
    lower = nodes // 2
    light = [k for k in ((n + lower // 2) % lower for n in range(lower)) if k] + [0]
    units = [[nodes - 1]]
    for n in range(1, lower):
        units += [[nodes - 1 - n], [light[n - 1]]]
    units.append([light[-1]])
    wait_for = {4: (0,), 5: (1,), 6: (2, 3)}
    blocks_of, far_blocks = [], []
    for unit in units:
        blocks_of.append(turn(own, arrived, unit, blocks_of[-1:]))
        far_blocks.append(lax.ppermute(blocks_of[-1], "ao", far))
    returned, made = {}, []
    for n, unit in enumerate(units):
        early = list(made[:1]) + [returned[k] for m in wait_for.get(n, ()) for k in units[m]]
        made = products(blocks_of[n], far_blocks[n], tiles_done, early)
        for k, x in zip(unit, made):
            returned[k] = lax.ppermute(x, "occ", [(o, o ^ k) for o in range(nodes)]) if k else x
    late = [returned[k] for m in (5, 4) if m < len(units) for k in units[m]]
    target_rows = rows_after(target_rows, late)
    returned = [returned[k] for k in range(nodes)]
    keep, give_up = back_transform(target_rows, returned)
    return jnp.swapaxes(keep + lax.ppermute(give_up, "ao", near), 1, 2)


def plain_shards(amplitudes, orbitals, tiles, tile_count, tile_row, tile_src, tile_sub):
    nodes = lax.axis_size("occ")
    parts = lax.axis_size("ao")
    part = lax.axis_index("ao")
    core = part % 2
    near = [(q, q ^ 1) for q in range(parts)]
    far = [(q, q ^ 2) for q in range(parts)]
    vir_part = amplitudes.shape[2]
    nu_part = tiles.shape[2]
    slots = tiles.shape[0]
    half = slots // 2
    blocks = orbitals.shape[0] // nodes
    pick = lax.dynamic_slice_in_dim
    ordered = jnp.concatenate([pick(orbitals, (part ^ q) * vir_part, vir_part, 1) for q in range(parts)], 1)
    side_rows = jnp.concatenate([pick(ordered, (part ^ q) * nu_part, nu_part, 0) for q in range(2)], 0)

    def mine_of(table):
        return pick(table.reshape(nodes, slots), core * half, half, 1)

    def product(form, a, b):
        return jnp.einsum(form, a, b, preferred_element_type=F32)

    def split(x, at, axis):
        size = x.shape[axis] // 2
        return pick(x, at * size, size, axis), pick(x, (1 - at) * size, size, axis)

    source = mine_of(tile_src[:, 0]) * blocks + mine_of(tile_sub)
    target = jnp.arange(nodes, dtype=jnp.int32)[:, None] * blocks + mine_of(tile_row)
    place = core * half + jnp.arange(half, dtype=jnp.int32)
    live = place[None, :] < tile_count[:, None]
    source_rows = jnp.take(orbitals, source, axis=0)
    target_rows = jnp.where(live[:, :, None], jnp.take(orbitals, target, axis=0), 0)
    paired = jnp.concatenate([amplitudes, lax.ppermute(amplitudes, "ao", near)], 2)
    sent = product("otc,icd->otid", source_rows, paired).astype(BF16)
    arrived = lax.all_to_all(sent, "occ", split_axis=0, concat_axis=0, tiled=True)
    keep, give = split(product("sb,tsn->tbn", orbitals, tiles).astype(BF16), core, 0)
    whole = jnp.concatenate([keep, lax.ppermute(give, "ao", near)], 2)
    both = product("tbn,nd->tbd", whole, side_rows).astype(BF16)
    dressed = both[:, :, :2 * vir_part] + lax.ppermute(both[:, :, 2 * vir_part:], "ao", far)
    both = product("otid,tbd->otib", arrived, dressed).astype(BF16)
    here, there = split(both, part // 2, 3)
    summed = here + lax.ppermute(there, "ao", far)
    back = lax.all_to_all(summed, "occ", split_axis=0, concat_axis=0, tiled=True)
    total = product("ota,otib->iab", target_rows, back).astype(BF16)
    keep, give = split(total, core, 2)
    return keep + lax.ppermute(give, "ao", near)


def solution(mesh):
    placed = (P("occ", None, "ao"), P(), P("occ", None, "ao"), P(), P(), P(), P())

    def whole(amplitudes, *rest):
        nodes = mesh.shape["occ"]
        rows = amplitudes.shape[0] // nodes
        few = nodes <= 16 and nodes & (nodes - 1) == 0
        body = shards if few and rows % 16 == 0 else plain_shards
        return jax.shard_map(
            body, mesh=mesh, in_specs=placed, out_specs=P("occ", None, "ao"), check_vma=False
        )(amplitudes, *rest)

    return whole
```

```python
import functools

import jax
import jax.numpy as jnp
from jax import lax
from jax.experimental import pallas as pl
from jax.experimental.pallas import tpu as pltpu
from jax.sharding import PartitionSpec as P

F32, BF16 = jnp.float32, jnp.bfloat16
TILE_PARTS = 4
VMEM_LIMIT = 16 * 1024 * 1024
TILE_VMEM_LIMIT = 50 * 1024 * 1024


def dot(a, b, dims=(((1,), (0,)), ((), ()))):
    return lax.dot_general(a, b, dims, preferred_element_type=F32)


def call(body, outs, ins, flops, scratch=(), early=(), limit=VMEM_LIMIT):
    whole = pl.BlockSpec(memory_space=pltpu.VMEM)
    moved = sum(2 * x.size for x in ins) + sum(2 * x.size for x in outs)
    return pl.pallas_call(
        body,
        out_shape=outs,
        in_specs=[whole] * len(ins) + [pl.BlockSpec(memory_space=pl.ANY)] * len(early),
        out_specs=[whole] * len(outs),
        scratch_shapes=list(scratch),
        cost_estimate=pl.CostEstimate(flops=flops, bytes_accessed=moved, transcendentals=0),
        compiler_params=pltpu.CompilerParams(vmem_limit_bytes=limit),
    )(*ins, *early)


def order_orbitals(orbitals, left, side_rows, held):
    vir = orbitals.shape[1]
    part = lax.axis_index("ao")
    nu_part = side_rows.shape[0] // 2
    line = orbitals[...]
    left[...] = line.T
    quarters = [line[:, q:q + vir // 4] for q in (vir // 4, 0, 3 * vir // 4, vir // 2)]
    line = jnp.where(part % 2 == 0, line, jnp.concatenate(quarters, 1))
    line = jnp.where(part // 2 == 0, line, jnp.concatenate([line[:, vir // 2:], line[:, :vir // 2]], 1))
    held[...] = line
    for q in range(2):
        start = pl.multiple_of((part ^ q) * nu_part, nu_part)
        side_rows[pl.ds(q * nu_part, nu_part), :] = held[pl.ds(start, nu_part), :]


def source_body(src, sub, orbitals, early, source, held, ahead):
    held[...] = orbitals[...].astype(F32)
    nodes = lax.axis_size("occ")
    slots = src.shape[0] // nodes
    half = slots // 2
    blocks = held.shape[0] // nodes
    core = lax.axis_index("ao") % 2
    for k in range(nodes):

        def step(j, carry):
            slot = k * slots + core * half + j
            ahead[pl.ds(k * half + j, 1), :] = held[pl.ds(src[slot] * blocks + sub[slot], 1), :]
            return carry

        lax.fori_loop(0, half, step, 0, unroll=8)
    source[...] = ahead[...].astype(BF16)


def target_body(row, count, orbitals, early, target, held, back):
    held[...] = orbitals[...].astype(F32)
    nodes = count.shape[0]
    slots = row.shape[0] // nodes
    half = slots // 2
    blocks = held.shape[0] // nodes
    own, core = lax.axis_index("occ"), lax.axis_index("ao") % 2
    for k in range(nodes):
        partner = own ^ k

        def step(j, carry):
            place = core * half + j
            line = held[pl.ds(partner * blocks + row[partner * slots + place], 1), :]
            back[pl.ds(k * half + j, 1), :] = jnp.where(place < count[partner], line, 0.0)
            return carry

        lax.fori_loop(0, half, step, 0, unroll=8)
    target[...] = back[...].astype(BF16)


def gather(body, tables, orbitals, early):
    slots, vir = tables[0].shape[0] // 2, orbitals.shape[1]
    scalar = pl.BlockSpec(memory_space=pltpu.SMEM)
    whole = pl.BlockSpec(memory_space=pltpu.VMEM)
    return pl.pallas_call(
        body,
        out_shape=jax.ShapeDtypeStruct((slots, vir), BF16),
        in_specs=[scalar] * 2 + [whole, pl.BlockSpec(memory_space=pl.ANY)],
        out_specs=whole,
        scratch_shapes=[pltpu.VMEM(orbitals.shape, F32), pltpu.VMEM((slots, vir), F32)],
        cost_estimate=pl.CostEstimate(flops=slots * vir, bytes_accessed=4 * slots * vir, transcendentals=0),
        compiler_params=pltpu.CompilerParams(vmem_limit_bytes=VMEM_LIMIT),
    )(*tables, orbitals, early)


def rows_body(rows_ref, mine_ref, other_ref, *rest):
    out, held, sems = rest[-3:]
    nodes, occ, slots, width = held.shape
    rows = rows_ref[...]
    copies = []
    part = occ // sems.shape[0]
    for s in range(sems.shape[0]):
        for i in range(s * part, (s + 1) * part, 2):
            right = jnp.concatenate([mine_ref[i], other_ref[i], mine_ref[i + 1], other_ref[i + 1]], 0)
            product = dot(rows, right, (((1,), (1,)), ((), ()))).astype(BF16)
            for j in range(2):
                held[:, i + j] = product[:, j * width:(j + 1) * width].reshape(nodes, slots, width)
        piece = pl.ds(s * part, part)
        copies.append(pltpu.make_async_copy(held.at[:, piece], out.at[:, piece], sems.at[s]))
        copies[-1].start()
    for copy in copies:
        copy.wait()


def pair_rows(rows, mine, other, nodes, early):
    occ, part, vir = mine.shape
    count = rows.shape[0]
    shape = (nodes, occ, count // nodes, 2 * part)
    whole = pl.BlockSpec(memory_space=pltpu.VMEM)
    away = pl.BlockSpec(memory_space=pl.ANY)
    return pl.pallas_call(
        rows_body,
        out_shape=jax.ShapeDtypeStruct(shape, BF16),
        in_specs=[whole] * 3 + [away] * len(early),
        out_specs=pl.BlockSpec(memory_space=pltpu.HBM),
        scratch_shapes=[pltpu.VMEM(shape, BF16), pltpu.SemaphoreType.DMA((8,))],
        cost_estimate=pl.CostEstimate(
            flops=4 * count * occ * vir * part, bytes_accessed=4 * occ * part * vir, transcendentals=0
        ),
        compiler_params=pltpu.CompilerParams(vmem_limit_bytes=TILE_VMEM_LIMIT),
    )(rows, mine, other, *early)


def turn_body(groups, meta, *refs):
    blocks, (out, held) = refs[:groups], refs[-2:]
    _, occ, slots, width = blocks[0].shape
    for n in range(groups):
        base = n * occ * slots
        held[base:base + occ * slots, :] = blocks[n][0].astype(F32).reshape(occ * slots, width)
        for t in range(slots):
            out[n, t] = held[pl.ds(base + t, occ, stride=slots), :].astype(BF16)


def turn(own, arrived, partners, early):
    groups = len(partners)
    _, occ, slots, width = arrived.shape
    specs = [
        pl.BlockSpec((1, occ, slots, width), lambda n, ref, k=k: (ref[0] ^ k, 0, 0, 0)) for k in partners
    ]
    return pl.pallas_call(
        functools.partial(turn_body, groups),
        out_shape=jax.ShapeDtypeStruct((groups, slots, occ, width), BF16),
        grid_spec=pltpu.PrefetchScalarGridSpec(
            num_scalar_prefetch=1,
            grid=(1,),
            in_specs=specs + [pl.BlockSpec(memory_space=pl.ANY)] * len(early),
            out_specs=pl.BlockSpec(memory_space=pltpu.VMEM),
            scratch_shapes=[pltpu.VMEM((groups * occ * slots, width), F32)],
        ),
        cost_estimate=pl.CostEstimate(
            flops=groups * occ * slots * width, bytes_accessed=4 * groups * occ * slots * width, transcendentals=0
        ),
        compiler_params=pltpu.CompilerParams(vmem_limit_bytes=VMEM_LIMIT),
    )(jnp.reshape(own, (1,)), *[arrived] * groups, *early)


def start_copies(other_core, start, tiles, held, sems):
    core = lax.axis_index("ao") % 2
    offset = (1 - core if other_core else core) * (tiles.shape[0] // 2) + start
    pieces = sems.shape[0]
    size = held.shape[0] // pieces
    copies = []
    for n in range(pieces):
        source = tiles.at[pl.ds(offset + n * size, size)]
        copies.append(pltpu.make_async_copy(source, held.at[pl.ds(n * size, size)], sems.at[n]))
        copies[n].start()
    return copies


def pair_dot(left, held, t):
    product = dot(left, jnp.concatenate([held[t], held[t + 1]], 1))
    width = held.shape[2]
    return product[:, :width].astype(BF16), product[:, width:].astype(BF16)


def transform_tiles(left_ref, copies, held, out):
    size = out.shape[0] // len(copies)
    left = left_ref[...]
    for n, copy in enumerate(copies):
        copy.wait()
        for t in range(n * size, (n + 1) * size, 2):
            out[t], out[t + 1] = pair_dot(left, held, t)


def give_kernel(start, left_ref, tiles, *rest):
    out, held, sems = rest[-3:]
    transform_tiles(left_ref, start_copies(True, start, tiles, held, sems), held, out)


def first_kernel(start, orbitals, tiles, out, left_ref, side_rows, held, sems, lines, whole, sem):
    fetch = pltpu.make_async_copy(orbitals, whole, sem)
    fetch.start()
    copies = start_copies(True, start, tiles, held, sems)
    fetch.wait()
    order_orbitals(whole, left_ref, side_rows, lines)
    transform_tiles(left_ref, copies, held, out)


def finish_kernel(start, skip, left_ref, tiles, other, right_ref, *rest):
    here, there, held, sems = rest[-4:]
    copies = start_copies(False, start, tiles, held, sems)
    size = here.shape[0] // len(copies)
    width = here.shape[1]
    left, right = left_ref[...], right_ref[...]
    side = lax.axis_index("ao") // 2
    for n, copy in enumerate(copies):
        copy.wait()
        rows = []
        for t in range(n * size, (n + 1) * size, 2):
            for j, mine in enumerate(pair_dot(left, held, t)):
                rows.append(jnp.concatenate([mine, other[skip + t + j]], 1))
        both = dot(jnp.concatenate(rows, 0), right).reshape(size, -1, right.shape[1]).astype(BF16)
        piece = pl.ds(n * size, size)
        low, high = both[:, :width], both[:, width:]
        here[piece] = jnp.where(side == 0, low, high)
        away = jnp.where(side == 0, high, low)
        there[piece] = jnp.concatenate([away[:, :, width:], away[:, :, :width]], 2)


PIECE = 8


def tile_call(body, count, tiles, ins, outs, early=(), scratch=(), first=None):
    _, sig, nu = tiles.shape
    vir = outs[0].shape[1]
    whole = pl.BlockSpec(memory_space=pltpu.VMEM)
    away = pl.BlockSpec(memory_space=pl.ANY)
    flops = 2 * count * vir * nu * (sig + 2 * vir * (len(outs) - 1))
    return pl.pallas_call(
        body,
        out_shape=outs,
        in_specs=[first or whole, away] + [whole] * (len(ins) - 1) + [away] * len(early),
        out_specs=[whole] * len(outs),
        scratch_shapes=[pltpu.VMEM((count, sig, nu), BF16), pltpu.SemaphoreType.DMA((count // PIECE,)), *scratch],
        cost_estimate=pl.CostEstimate(
            flops=flops, bytes_accessed=2 * count * sig * nu * 2, transcendentals=0
        ),
        compiler_params=pltpu.CompilerParams(vmem_limit_bytes=TILE_VMEM_LIMIT),
    )(ins[0], tiles, *ins[1:], *early)


def dress_body(parts, *refs):
    out = refs[-1]
    t = 0
    for n in range(parts):
        size = refs[2 * n].shape[0]
        out[t:t + size] = refs[2 * n][...] + refs[2 * n + 1][...]
        t += size


def dress(parts):
    slots = sum(x.shape[0] for x in parts[::2])
    outs = [jax.ShapeDtypeStruct((slots,) + parts[0].shape[1:], BF16)]
    return call(functools.partial(dress_body, len(parts) // 2), outs, parts, slots)[0]


def product_body(near_ref, far_ref, dressed, last, last_far, *refs):
    scratch = refs[-1]
    groups, slots, occ, _ = near_ref.shape
    outs = refs[-1 - groups:-1]
    first = dressed.shape[0]
    for t in range(slots):
        tile = dressed[t] if t < first else last[t - first] + last_far[t - first]
        rows = [jnp.concatenate([near_ref[n, t], far_ref[n, t]], 1) for n in range(groups)]
        product = dot(jnp.concatenate(rows, 0), tile, (((1,), (1,)), ((), ())))
        scratch[pl.ds(t, groups * occ, stride=slots), :] = product
    for n, out in enumerate(outs):
        block = occ * slots
        out[...] = scratch[n * block:(n + 1) * block, :].reshape(out.shape).astype(BF16)


def products(near_rows, far_rows, tiles, early):
    groups, slots, occ, width = near_rows.shape
    outs = [jax.ShapeDtypeStruct((occ, slots, width), BF16)] * groups
    scratch = [pltpu.VMEM((groups * occ * slots, width), F32)]
    flops = 4 * groups * occ * slots * width * width
    return call(product_body, outs, (near_rows, far_rows, *tiles), flops, scratch, early)


def copy_body(rows, *rest):
    rest[-1][...] = rows[...]


def rows_after(rows, early):
    return call(copy_body, [jax.ShapeDtypeStruct(rows.shape, BF16)], (rows,), rows.size, (), early)[0]


def back_body(nodes, rows_ref, *refs):
    values, (keep, give) = refs[:nodes], refs[nodes:]
    occ = values[0].shape[0]
    part = keep.shape[1]
    core = lax.axis_index("ao") % 2
    rows = rows_ref[...]

    def step(i, carry):
        left = jnp.concatenate([v[i] for v in values], 0)
        product = dot(left, rows, (((0,), (0,)), ((), ())))
        low, high = product[:part].astype(BF16), product[part:].astype(BF16)
        keep[i] = jnp.where(core == 0, low, high)
        give[i] = jnp.where(core == 0, high, low)
        return carry

    lax.fori_loop(0, occ, step, 0, unroll=16)


def back_transform(rows, values):
    occ, _, width = values[0].shape
    count, vir = rows.shape
    outs = [jax.ShapeDtypeStruct((occ, width // 2, vir), BF16)] * 2
    return call(
        functools.partial(back_body, len(values)), outs, (rows, *values), 2 * occ * vir * count * width
    )


def shards(amplitudes, orbitals, tiles, tile_count, tile_row, tile_src, tile_sub):
    nodes = lax.axis_size("occ")
    own = lax.axis_index("occ")
    parts = lax.axis_size("ao")
    part = lax.axis_index("ao")
    core = part % 2
    near = [(q, q ^ 1) for q in range(parts)]
    far = [(q, q ^ 2) for q in range(parts)]
    local_occ, vir, vir_part = amplitudes.shape
    nu_part = tiles.shape[2]
    slots = tiles.shape[0]
    half = slots // 2
    blocks = orbitals.shape[0] // nodes
    pick = lax.dynamic_slice_in_dim

    mine = jnp.swapaxes(amplitudes, 1, 2)
    other = lax.ppermute(mine, "ao", near)
    def tile_shape(count, width):
        return jax.ShapeDtypeStruct((count, vir, width), BF16)

    def give(start, early):
        outs = [tile_shape(half // 2, nu_part)]
        body = functools.partial(give_kernel, start)
        (given,) = tile_call(body, half // 2, tiles, (left,), outs, early)
        return given, lax.ppermute(given, "ao", near)

    outs = [
        tile_shape(half // 2, nu_part),
        jax.ShapeDtypeStruct((vir, orbitals.shape[0]), BF16),
        jax.ShapeDtypeStruct((2 * nu_part, vir), BF16),
    ]
    scratch = [pltpu.VMEM(orbitals.shape, BF16)] * 2 + [pltpu.SemaphoreType.DMA]
    given, left, side_rows = tile_call(
        functools.partial(first_kernel, 0), half // 2, tiles, (orbitals,), outs, (), scratch,
        pl.BlockSpec(memory_space=pltpu.HBM),
    )
    first_parts = lax.ppermute(given, "ao", near)
    given, second_parts = give(half // 2, [given, other])
    source_rows = gather(source_body, (tile_src[:, 0], tile_sub), orbitals, given)
    sent = pair_rows(source_rows, mine, other, nodes, (first_parts, second_parts))
    arrived = lax.all_to_all(sent, "occ", split_axis=0, concat_axis=0, tiled=True)
    parts, early = [], [sent]
    step = half // TILE_PARTS
    for n in range(TILE_PARTS):
        if n >= 2:
            early.append(parts[2 * n - 3])
        other_parts = first_parts if 2 * n < TILE_PARTS else second_parts
        here, there = tile_call(
            functools.partial(finish_kernel, n * step, n * step % (half // 2)), step, tiles,
            (left, other_parts, side_rows), [jax.ShapeDtypeStruct((step, vir // 2, vir), BF16)] * 2, early,
        )
        early = [there]
        parts += [here, lax.ppermute(there, "ao", far)]
    target_rows = gather(target_body, (tile_row, tile_count), orbitals, early[0])
    tiles_done = [dress(parts[:-2]), *parts[-2:]]
    lower = nodes // 2
    light = [k for k in ((n + lower // 2) % lower for n in range(lower)) if k] + [0]
    units = [[nodes - 1]]
    for n in range(1, lower):
        units += [[nodes - 1 - n], [light[n - 1]]]
    units.append([light[-1]])
    wait_for = {4: (0,), 5: (1,), 6: (2, 3)}
    blocks_of, far_blocks = [], []
    for unit in units:
        blocks_of.append(turn(own, arrived, unit, blocks_of[-1:]))
        far_blocks.append(lax.ppermute(blocks_of[-1], "ao", far))
    returned, made = {}, []
    for n, unit in enumerate(units):
        early = list(made[:1]) + [returned[k] for m in wait_for.get(n, ()) for k in units[m]]
        made = products(blocks_of[n], far_blocks[n], tiles_done, early)
        for k, x in zip(unit, made):
            returned[k] = lax.ppermute(x, "occ", [(o, o ^ k) for o in range(nodes)]) if k else x
    late = [returned[k] for m in (5, 4) if m < len(units) for k in units[m]]
    target_rows = rows_after(target_rows, late)
    returned = [returned[k] for k in range(nodes)]
    keep, give_up = back_transform(target_rows, returned)
    return jnp.swapaxes(keep + lax.ppermute(give_up, "ao", near), 1, 2)


def plain_shards(amplitudes, orbitals, tiles, tile_count, tile_row, tile_src, tile_sub):
    nodes = lax.axis_size("occ")
    parts = lax.axis_size("ao")
    part = lax.axis_index("ao")
    core = part % 2
    near = [(q, q ^ 1) for q in range(parts)]
    far = [(q, q ^ 2) for q in range(parts)]
    vir_part = amplitudes.shape[2]
    nu_part = tiles.shape[2]
    slots = tiles.shape[0]
    half = slots // 2
    blocks = orbitals.shape[0] // nodes
    pick = lax.dynamic_slice_in_dim
    ordered = jnp.concatenate([pick(orbitals, (part ^ q) * vir_part, vir_part, 1) for q in range(parts)], 1)
    side_rows = jnp.concatenate([pick(ordered, (part ^ q) * nu_part, nu_part, 0) for q in range(2)], 0)

    def mine_of(table):
        return pick(table.reshape(nodes, slots), core * half, half, 1)

    def product(form, a, b):
        return jnp.einsum(form, a, b, preferred_element_type=F32)

    def split(x, at, axis):
        size = x.shape[axis] // 2
        return pick(x, at * size, size, axis), pick(x, (1 - at) * size, size, axis)

    source = mine_of(tile_src[:, 0]) * blocks + mine_of(tile_sub)
    target = jnp.arange(nodes, dtype=jnp.int32)[:, None] * blocks + mine_of(tile_row)
    place = core * half + jnp.arange(half, dtype=jnp.int32)
    live = place[None, :] < tile_count[:, None]
    source_rows = jnp.take(orbitals, source, axis=0)
    target_rows = jnp.where(live[:, :, None], jnp.take(orbitals, target, axis=0), 0)
    paired = jnp.concatenate([amplitudes, lax.ppermute(amplitudes, "ao", near)], 2)
    sent = product("otc,icd->otid", source_rows, paired).astype(BF16)
    arrived = lax.all_to_all(sent, "occ", split_axis=0, concat_axis=0, tiled=True)
    keep, give = split(product("sb,tsn->tbn", orbitals, tiles).astype(BF16), core, 0)
    whole = jnp.concatenate([keep, lax.ppermute(give, "ao", near)], 2)
    both = product("tbn,nd->tbd", whole, side_rows).astype(BF16)
    dressed = both[:, :, :2 * vir_part] + lax.ppermute(both[:, :, 2 * vir_part:], "ao", far)
    both = product("otid,tbd->otib", arrived, dressed).astype(BF16)
    here, there = split(both, part // 2, 3)
    summed = here + lax.ppermute(there, "ao", far)
    back = lax.all_to_all(summed, "occ", split_axis=0, concat_axis=0, tiled=True)
    total = product("ota,otib->iab", target_rows, back).astype(BF16)
    keep, give = split(total, core, 2)
    return keep + lax.ppermute(give, "ao", near)


def solution(mesh):
    placed = (P("occ", None, "ao"), P(), P("occ", None, "ao"), P(), P(), P(), P())

    def whole(amplitudes, *rest):
        nodes = mesh.shape["occ"]
        rows = amplitudes.shape[0] // nodes
        few = nodes <= 16 and nodes & (nodes - 1) == 0
        body = shards if few and rows % 16 == 0 else plain_shards
        return jax.shard_map(
            body, mesh=mesh, in_specs=placed, out_specs=P("occ", None, "ao"), check_vma=False
        )(amplitudes, *rest)

    return whole
```

```python
import functools

import jax
import jax.numpy as jnp
from jax import lax
from jax.experimental import pallas as pl
from jax.experimental.pallas import tpu as pltpu
from jax.sharding import PartitionSpec as P

F32, BF16 = jnp.float32, jnp.bfloat16
TILE_PARTS = 4
VMEM_LIMIT = 16 * 1024 * 1024
TILE_VMEM_LIMIT = 50 * 1024 * 1024


def dot(a, b, dims=(((1,), (0,)), ((), ()))):
    return lax.dot_general(a, b, dims, preferred_element_type=F32)


def call(body, outs, ins, flops, scratch=(), early=(), limit=VMEM_LIMIT):
    whole = pl.BlockSpec(memory_space=pltpu.VMEM)
    moved = sum(2 * x.size for x in ins) + sum(2 * x.size for x in outs)
    return pl.pallas_call(
        body,
        out_shape=outs,
        in_specs=[whole] * len(ins) + [pl.BlockSpec(memory_space=pl.ANY)] * len(early),
        out_specs=[whole] * len(outs),
        scratch_shapes=list(scratch),
        cost_estimate=pl.CostEstimate(flops=flops, bytes_accessed=moved, transcendentals=0),
        compiler_params=pltpu.CompilerParams(vmem_limit_bytes=limit),
    )(*ins, *early)


def order_orbitals(orbitals, left, side_rows, held):
    vir = orbitals.shape[1]
    part = lax.axis_index("ao")
    nu_part = side_rows.shape[0] // 2
    line = orbitals[...]
    left[...] = line.T
    quarters = [line[:, q:q + vir // 4] for q in (vir // 4, 0, 3 * vir // 4, vir // 2)]
    line = jnp.where(part % 2 == 0, line, jnp.concatenate(quarters, 1))
    line = jnp.where(part // 2 == 0, line, jnp.concatenate([line[:, vir // 2:], line[:, :vir // 2]], 1))
    held[...] = line
    for q in range(2):
        start = pl.multiple_of((part ^ q) * nu_part, nu_part)
        side_rows[pl.ds(q * nu_part, nu_part), :] = held[pl.ds(start, nu_part), :]


def source_body(src, sub, orbitals, early, source, held, ahead):
    held[...] = orbitals[...].astype(F32)
    nodes = lax.axis_size("occ")
    slots = src.shape[0] // nodes
    half = slots // 2
    blocks = held.shape[0] // nodes
    core = lax.axis_index("ao") % 2
    for k in range(nodes):

        def step(j, carry):
            slot = k * slots + core * half + j
            ahead[pl.ds(k * half + j, 1), :] = held[pl.ds(src[slot] * blocks + sub[slot], 1), :]
            return carry

        lax.fori_loop(0, half, step, 0, unroll=8)
    source[...] = ahead[...].astype(BF16)


def target_body(row, count, orbitals, early, target, held, back):
    held[...] = orbitals[...].astype(F32)
    nodes = count.shape[0]
    slots = row.shape[0] // nodes
    half = slots // 2
    blocks = held.shape[0] // nodes
    own, core = lax.axis_index("occ"), lax.axis_index("ao") % 2
    for k in range(nodes):
        partner = own ^ k

        def step(j, carry):
            place = core * half + j
            line = held[pl.ds(partner * blocks + row[partner * slots + place], 1), :]
            back[pl.ds(k * half + j, 1), :] = jnp.where(place < count[partner], line, 0.0)
            return carry

        lax.fori_loop(0, half, step, 0, unroll=8)
    target[...] = back[...].astype(BF16)


def gather(body, tables, orbitals, early):
    slots, vir = tables[0].shape[0] // 2, orbitals.shape[1]
    scalar = pl.BlockSpec(memory_space=pltpu.SMEM)
    whole = pl.BlockSpec(memory_space=pltpu.VMEM)
    return pl.pallas_call(
        body,
        out_shape=jax.ShapeDtypeStruct((slots, vir), BF16),
        in_specs=[scalar] * 2 + [whole, pl.BlockSpec(memory_space=pl.ANY)],
        out_specs=whole,
        scratch_shapes=[pltpu.VMEM(orbitals.shape, F32), pltpu.VMEM((slots, vir), F32)],
        cost_estimate=pl.CostEstimate(flops=slots * vir, bytes_accessed=4 * slots * vir, transcendentals=0),
        compiler_params=pltpu.CompilerParams(vmem_limit_bytes=VMEM_LIMIT),
    )(*tables, orbitals, early)


def rows_body(rows_ref, mine_ref, other_ref, *rest):
    out, held, sems = rest[-3:]
    nodes, occ, slots, width = held.shape
    rows = rows_ref[...]
    copies = []
    part = occ // sems.shape[0]
    for s in range(sems.shape[0]):
        for i in range(s * part, (s + 1) * part, 2):
            right = jnp.concatenate([mine_ref[i], other_ref[i], mine_ref[i + 1], other_ref[i + 1]], 0)
            product = dot(rows, right, (((1,), (1,)), ((), ()))).astype(BF16)
            for j in range(2):
                held[:, i + j] = product[:, j * width:(j + 1) * width].reshape(nodes, slots, width)
        piece = pl.ds(s * part, part)
        copies.append(pltpu.make_async_copy(held.at[:, piece], out.at[:, piece], sems.at[s]))
        copies[-1].start()
    for copy in copies:
        copy.wait()


def pair_rows(rows, mine, other, nodes, early):
    occ, part, vir = mine.shape
    count = rows.shape[0]
    shape = (nodes, occ, count // nodes, 2 * part)
    whole = pl.BlockSpec(memory_space=pltpu.VMEM)
    away = pl.BlockSpec(memory_space=pl.ANY)
    return pl.pallas_call(
        rows_body,
        out_shape=jax.ShapeDtypeStruct(shape, BF16),
        in_specs=[whole] * 3 + [away] * len(early),
        out_specs=pl.BlockSpec(memory_space=pltpu.HBM),
        scratch_shapes=[pltpu.VMEM(shape, BF16), pltpu.SemaphoreType.DMA((8,))],
        cost_estimate=pl.CostEstimate(
            flops=4 * count * occ * vir * part, bytes_accessed=4 * occ * part * vir, transcendentals=0
        ),
        compiler_params=pltpu.CompilerParams(vmem_limit_bytes=TILE_VMEM_LIMIT),
    )(rows, mine, other, *early)


def turn_body(groups, meta, *refs):
    blocks, (out, held) = refs[:groups], refs[-2:]
    _, occ, slots, width = blocks[0].shape
    for n in range(groups):
        base = n * occ * slots
        held[base:base + occ * slots, :] = blocks[n][0].astype(F32).reshape(occ * slots, width)
        for t in range(slots):
            out[n, t] = held[pl.ds(base + t, occ, stride=slots), :].astype(BF16)


def turn(own, arrived, partners, early):
    groups = len(partners)
    _, occ, slots, width = arrived.shape
    specs = [
        pl.BlockSpec((1, occ, slots, width), lambda n, ref, k=k: (ref[0] ^ k, 0, 0, 0)) for k in partners
    ]
    return pl.pallas_call(
        functools.partial(turn_body, groups),
        out_shape=jax.ShapeDtypeStruct((groups, slots, occ, width), BF16),
        grid_spec=pltpu.PrefetchScalarGridSpec(
            num_scalar_prefetch=1,
            grid=(1,),
            in_specs=specs + [pl.BlockSpec(memory_space=pl.ANY)] * len(early),
            out_specs=pl.BlockSpec(memory_space=pltpu.VMEM),
            scratch_shapes=[pltpu.VMEM((groups * occ * slots, width), F32)],
        ),
        cost_estimate=pl.CostEstimate(
            flops=groups * occ * slots * width, bytes_accessed=4 * groups * occ * slots * width, transcendentals=0
        ),
        compiler_params=pltpu.CompilerParams(vmem_limit_bytes=VMEM_LIMIT),
    )(jnp.reshape(own, (1,)), *[arrived] * groups, *early)


def start_copies(other_core, start, tiles, held, sems):
    core = lax.axis_index("ao") % 2
    offset = (1 - core if other_core else core) * (tiles.shape[0] // 2) + start
    pieces = sems.shape[0]
    size = held.shape[0] // pieces
    copies = []
    for n in range(pieces):
        source = tiles.at[pl.ds(offset + n * size, size)]
        copies.append(pltpu.make_async_copy(source, held.at[pl.ds(n * size, size)], sems.at[n]))
        copies[n].start()
    return copies


def pair_dot(left, held, t):
    product = dot(left, jnp.concatenate([held[t], held[t + 1]], 1))
    width = held.shape[2]
    return product[:, :width].astype(BF16), product[:, width:].astype(BF16)


def transform_tiles(left_ref, copies, held, out):
    size = out.shape[0] // len(copies)
    left = left_ref[...]
    for n, copy in enumerate(copies):
        copy.wait()
        for t in range(n * size, (n + 1) * size, 2):
            out[t], out[t + 1] = pair_dot(left, held, t)


def give_kernel(start, left_ref, tiles, *rest):
    out, held, sems = rest[-3:]
    transform_tiles(left_ref, start_copies(True, start, tiles, held, sems), held, out)


def first_kernel(start, orbitals, tiles, out, left_ref, side_rows, held, sems, lines, whole, sem):
    fetch = pltpu.make_async_copy(orbitals, whole, sem)
    fetch.start()
    copies = start_copies(True, start, tiles, held, sems)
    fetch.wait()
    order_orbitals(whole, left_ref, side_rows, lines)
    transform_tiles(left_ref, copies, held, out)


def finish_kernel(start, skip, left_ref, tiles, other, right_ref, *rest):
    here, there, held, sems = rest[-4:]
    copies = start_copies(False, start, tiles, held, sems)
    size = here.shape[0] // len(copies)
    width = here.shape[1]
    left, right = left_ref[...], right_ref[...]
    side = lax.axis_index("ao") // 2
    for n, copy in enumerate(copies):
        copy.wait()
        rows = []
        for t in range(n * size, (n + 1) * size, 2):
            for j, mine in enumerate(pair_dot(left, held, t)):
                rows.append(jnp.concatenate([mine, other[skip + t + j]], 1))
        both = dot(jnp.concatenate(rows, 0), right).reshape(size, -1, right.shape[1]).astype(BF16)
        piece = pl.ds(n * size, size)
        low, high = both[:, :width], both[:, width:]
        here[piece] = jnp.where(side == 0, low, high)
        away = jnp.where(side == 0, high, low)
        there[piece] = jnp.concatenate([away[:, :, width:], away[:, :, :width]], 2)


PIECE = 8


def tile_call(body, count, tiles, ins, outs, early=(), scratch=(), first=None):
    _, sig, nu = tiles.shape
    vir = outs[0].shape[1]
    whole = pl.BlockSpec(memory_space=pltpu.VMEM)
    away = pl.BlockSpec(memory_space=pl.ANY)
    flops = 2 * count * vir * nu * (sig + 2 * vir * (len(outs) - 1))
    return pl.pallas_call(
        body,
        out_shape=outs,
        in_specs=[first or whole, away] + [whole] * (len(ins) - 1) + [away] * len(early),
        out_specs=[whole] * len(outs),
        scratch_shapes=[pltpu.VMEM((count, sig, nu), BF16), pltpu.SemaphoreType.DMA((count // PIECE,)), *scratch],
        cost_estimate=pl.CostEstimate(
            flops=flops, bytes_accessed=2 * count * sig * nu * 2, transcendentals=0
        ),
        compiler_params=pltpu.CompilerParams(vmem_limit_bytes=TILE_VMEM_LIMIT),
    )(ins[0], tiles, *ins[1:], *early)


def dress_body(parts, *refs):
    out = refs[-1]
    t = 0
    for n in range(parts):
        size = refs[2 * n].shape[0]
        out[t:t + size] = refs[2 * n][...] + refs[2 * n + 1][...]
        t += size


def dress(parts):
    slots = sum(x.shape[0] for x in parts[::2])
    outs = [jax.ShapeDtypeStruct((slots,) + parts[0].shape[1:], BF16)]
    return call(functools.partial(dress_body, len(parts) // 2), outs, parts, slots)[0]


def product_body(near_ref, far_ref, dressed, last, last_far, *refs):
    scratch = refs[-1]
    groups, slots, occ, _ = near_ref.shape
    outs = refs[-1 - groups:-1]
    first = dressed.shape[0]
    for t in range(slots):
        tile = dressed[t] if t < first else last[t - first] + last_far[t - first]
        rows = [jnp.concatenate([near_ref[n, t], far_ref[n, t]], 1) for n in range(groups)]
        product = dot(jnp.concatenate(rows, 0), tile, (((1,), (1,)), ((), ())))
        scratch[pl.ds(t, groups * occ, stride=slots), :] = product
    for n, out in enumerate(outs):
        block = occ * slots
        out[...] = scratch[n * block:(n + 1) * block, :].reshape(out.shape).astype(BF16)


def products(near_rows, far_rows, tiles, early):
    groups, slots, occ, width = near_rows.shape
    outs = [jax.ShapeDtypeStruct((occ, slots, width), BF16)] * groups
    scratch = [pltpu.VMEM((groups * occ * slots, width), F32)]
    flops = 4 * groups * occ * slots * width * width
    return call(product_body, outs, (near_rows, far_rows, *tiles), flops, scratch, early)


def copy_body(rows, *rest):
    rest[-1][...] = rows[...]


def rows_after(rows, early):
    return call(copy_body, [jax.ShapeDtypeStruct(rows.shape, BF16)], (rows,), rows.size, (), early)[0]


def back_body(nodes, rows_ref, *refs):
    values, (keep, give) = refs[:nodes], refs[nodes:]
    occ = values[0].shape[0]
    part = keep.shape[1]
    core = lax.axis_index("ao") % 2
    rows = rows_ref[...]

    def step(i, carry):
        left = jnp.concatenate([v[i] for v in values], 0)
        product = dot(left, rows, (((0,), (0,)), ((), ())))
        low, high = product[:part].astype(BF16), product[part:].astype(BF16)
        keep[i] = jnp.where(core == 0, low, high)
        give[i] = jnp.where(core == 0, high, low)
        return carry

    lax.fori_loop(0, occ, step, 0, unroll=32)


def back_transform(rows, values):
    occ, _, width = values[0].shape
    count, vir = rows.shape
    outs = [jax.ShapeDtypeStruct((occ, width // 2, vir), BF16)] * 2
    return call(
        functools.partial(back_body, len(values)), outs, (rows, *values), 2 * occ * vir * count * width
    )


def shards(amplitudes, orbitals, tiles, tile_count, tile_row, tile_src, tile_sub):
    nodes = lax.axis_size("occ")
    own = lax.axis_index("occ")
    parts = lax.axis_size("ao")
    part = lax.axis_index("ao")
    core = part % 2
    near = [(q, q ^ 1) for q in range(parts)]
    far = [(q, q ^ 2) for q in range(parts)]
    local_occ, vir, vir_part = amplitudes.shape
    nu_part = tiles.shape[2]
    slots = tiles.shape[0]
    half = slots // 2
    blocks = orbitals.shape[0] // nodes
    pick = lax.dynamic_slice_in_dim

    mine = jnp.swapaxes(amplitudes, 1, 2)
    other = lax.ppermute(mine, "ao", near)
    def tile_shape(count, width):
        return jax.ShapeDtypeStruct((count, vir, width), BF16)

    def give(start, early):
        outs = [tile_shape(half // 2, nu_part)]
        body = functools.partial(give_kernel, start)
        (given,) = tile_call(body, half // 2, tiles, (left,), outs, early)
        return given, lax.ppermute(given, "ao", near)

    outs = [
        tile_shape(half // 2, nu_part),
        jax.ShapeDtypeStruct((vir, orbitals.shape[0]), BF16),
        jax.ShapeDtypeStruct((2 * nu_part, vir), BF16),
    ]
    scratch = [pltpu.VMEM(orbitals.shape, BF16)] * 2 + [pltpu.SemaphoreType.DMA]
    given, left, side_rows = tile_call(
        functools.partial(first_kernel, 0), half // 2, tiles, (orbitals,), outs, (), scratch,
        pl.BlockSpec(memory_space=pltpu.HBM),
    )
    first_parts = lax.ppermute(given, "ao", near)
    given, second_parts = give(half // 2, [given, other])
    source_rows = gather(source_body, (tile_src[:, 0], tile_sub), orbitals, given)
    sent = pair_rows(source_rows, mine, other, nodes, (first_parts, second_parts))
    arrived = lax.all_to_all(sent, "occ", split_axis=0, concat_axis=0, tiled=True)
    parts, early = [], [sent]
    step = half // TILE_PARTS
    for n in range(TILE_PARTS):
        if n >= 2:
            early.append(parts[2 * n - 3])
        other_parts = first_parts if 2 * n < TILE_PARTS else second_parts
        here, there = tile_call(
            functools.partial(finish_kernel, n * step, n * step % (half // 2)), step, tiles,
            (left, other_parts, side_rows), [jax.ShapeDtypeStruct((step, vir // 2, vir), BF16)] * 2, early,
        )
        early = [there]
        parts += [here, lax.ppermute(there, "ao", far)]
    target_rows = gather(target_body, (tile_row, tile_count), orbitals, early[0])
    tiles_done = [dress(parts[:-2]), *parts[-2:]]
    lower = nodes // 2
    light = [k for k in ((n + lower // 2) % lower for n in range(lower)) if k] + [0]
    units = [[nodes - 1]]
    for n in range(1, lower):
        units += [[nodes - 1 - n], [light[n - 1]]]
    units.append([light[-1]])
    wait_for = {4: (0,), 5: (1,), 6: (2, 3)}
    blocks_of, far_blocks = [], []
    for unit in units:
        blocks_of.append(turn(own, arrived, unit, blocks_of[-1:]))
        far_blocks.append(lax.ppermute(blocks_of[-1], "ao", far))
    returned, made = {}, []
    for n, unit in enumerate(units):
        early = list(made[:1]) + [returned[k] for m in wait_for.get(n, ()) for k in units[m]]
        made = products(blocks_of[n], far_blocks[n], tiles_done, early)
        for k, x in zip(unit, made):
            returned[k] = lax.ppermute(x, "occ", [(o, o ^ k) for o in range(nodes)]) if k else x
    late = [returned[k] for m in (5, 4) if m < len(units) for k in units[m]]
    target_rows = rows_after(target_rows, late)
    returned = [returned[k] for k in range(nodes)]
    keep, give_up = back_transform(target_rows, returned)
    return jnp.swapaxes(keep + lax.ppermute(give_up, "ao", near), 1, 2)


def plain_shards(amplitudes, orbitals, tiles, tile_count, tile_row, tile_src, tile_sub):
    nodes = lax.axis_size("occ")
    parts = lax.axis_size("ao")
    part = lax.axis_index("ao")
    core = part % 2
    near = [(q, q ^ 1) for q in range(parts)]
    far = [(q, q ^ 2) for q in range(parts)]
    vir_part = amplitudes.shape[2]
    nu_part = tiles.shape[2]
    slots = tiles.shape[0]
    half = slots // 2
    blocks = orbitals.shape[0] // nodes
    pick = lax.dynamic_slice_in_dim
    ordered = jnp.concatenate([pick(orbitals, (part ^ q) * vir_part, vir_part, 1) for q in range(parts)], 1)
    side_rows = jnp.concatenate([pick(ordered, (part ^ q) * nu_part, nu_part, 0) for q in range(2)], 0)

    def mine_of(table):
        return pick(table.reshape(nodes, slots), core * half, half, 1)

    def product(form, a, b):
        return jnp.einsum(form, a, b, preferred_element_type=F32)

    def split(x, at, axis):
        size = x.shape[axis] // 2
        return pick(x, at * size, size, axis), pick(x, (1 - at) * size, size, axis)

    source = mine_of(tile_src[:, 0]) * blocks + mine_of(tile_sub)
    target = jnp.arange(nodes, dtype=jnp.int32)[:, None] * blocks + mine_of(tile_row)
    place = core * half + jnp.arange(half, dtype=jnp.int32)
    live = place[None, :] < tile_count[:, None]
    source_rows = jnp.take(orbitals, source, axis=0)
    target_rows = jnp.where(live[:, :, None], jnp.take(orbitals, target, axis=0), 0)
    paired = jnp.concatenate([amplitudes, lax.ppermute(amplitudes, "ao", near)], 2)
    sent = product("otc,icd->otid", source_rows, paired).astype(BF16)
    arrived = lax.all_to_all(sent, "occ", split_axis=0, concat_axis=0, tiled=True)
    keep, give = split(product("sb,tsn->tbn", orbitals, tiles).astype(BF16), core, 0)
    whole = jnp.concatenate([keep, lax.ppermute(give, "ao", near)], 2)
    both = product("tbn,nd->tbd", whole, side_rows).astype(BF16)
    dressed = both[:, :, :2 * vir_part] + lax.ppermute(both[:, :, 2 * vir_part:], "ao", far)
    both = product("otid,tbd->otib", arrived, dressed).astype(BF16)
    here, there = split(both, part // 2, 3)
    summed = here + lax.ppermute(there, "ao", far)
    back = lax.all_to_all(summed, "occ", split_axis=0, concat_axis=0, tiled=True)
    total = product("ota,otib->iab", target_rows, back).astype(BF16)
    keep, give = split(total, core, 2)
    return keep + lax.ppermute(give, "ao", near)


def solution(mesh):
    placed = (P("occ", None, "ao"), P(), P("occ", None, "ao"), P(), P(), P(), P())

    def whole(amplitudes, *rest):
        nodes = mesh.shape["occ"]
        rows = amplitudes.shape[0] // nodes
        few = nodes <= 16 and nodes & (nodes - 1) == 0
        body = shards if few and rows % 16 == 0 else plain_shards
        return jax.shard_map(
            body, mesh=mesh, in_specs=placed, out_specs=P("occ", None, "ao"), check_vma=False
        )(amplitudes, *rest)

    return whole
```
